256 devices in a mesh: dp: 32 (over y, z), tensor: 8 (over x, core).
Axes of the slice: x: 4, y: 4, z: 8, core: 2. Of those that a mesh axis runs over, the one named last changes fastest.
Arguments:
- pixels: bfloat16 [32, 256, 128], P(None, ('dp', 'tensor')), may hold values from -6 to 6
- counts: int32 [32], replicated, may hold values from 1 to 8, as said below
- var_ids: int32 [32, 8], replicated, may hold values from 0 to 47, as said below
- destination: int32 [32], replicated, may hold values from 0 to 31, each once
- embed_weight: bfloat16 [48, 16, 4096], P(None, None, 'tensor'), may hold values from -1.5 to 1.5
- var_embed: bfloat16 [48, 4096], P(None, 'tensor'), may hold values from -4 to 4
- agg_query: bfloat16 [4096], P('tensor'), may hold values from -200 to 200
- ln_gain: bfloat16 [1, 4096], P(None, 'tensor'), may hold values from 0.25 to 1.75
- fc_up: bfloat16 [4096, 8192], P(None, 'tensor'), may hold values from -0.09375 to 0.09375
- fc_down: bfloat16 [4096, 8192], P('dp', 'tensor'), may hold values from -0.0625 to 0.0625
- cotangent: bfloat16 [32, 256, 4096], P('dp', None, 'tensor'), may hold values from -6 to 6
Outputs:
- mixed: bfloat16 [32, 256, 4096], P('dp', None, 'tensor')
- grad_embed: float32 [48, 16, 4096], P(None, None, 'tensor')
- grad_var: float32 [48, 4096], P(None, 'tensor')
- grad_query: float32 [4096], P('tensor')
The draws below stay inside these ranges and needn't reach their ends.
Inputs may be any that keep to these rules, and one draw needn't show every extreme that they name: `counts`: some sample has 8 live variables in every draw. `var_ids`: the ids of one sample's slots are distinct. `destination`: each rank is named once.
All inputs are finite; a program needn't handle non-finite values.
Results may differ from the reference program's by a relative error of at most 0.017.
The reference program's roundings to bfloat16 on the way count: a program that leaves them out, or rounds other values in their place, can miss the bound.
Values may be sent and summed in bfloat16 or wider, within the bound.
No kernel may reach another device: no remote copies, remote signals or barrier semaphores. Data moves between devices by JAX's collectives and lax.ppermute only.
A program may use at most 128 MiB of HBM per device.

```python
import jax
import jax.numpy as jnp
from jax import lax

D = 4096
HEADS = 32
HEAD = 128
FF = 8192
NVAR = 48
VMAX = 8
PP = 16
PATCHES = 256
SAMPLES = 32
N_DP = 32


def draw_counts(key, part):
    key = jax.random.fold_in(key, 11)
    first_key, second_key = jax.random.split(key)
    first_draw = jax.random.randint(first_key, (SAMPLES,), 1, VMAX + 1)
    full_index = jax.random.randint(second_key, (), 0, SAMPLES)
    return first_draw.at[full_index].set(VMAX).astype(jnp.int32)


def draw_var_ids(key, part):
    key = jax.random.fold_in(key, 23)
    row_keys = jax.random.split(key, SAMPLES)

    def one_row(row_key):
        return jax.random.permutation(row_key, NVAR)[:VMAX]
    return jax.vmap(one_row)(row_keys).astype(jnp.int32)


def query_values(key, lowest, highest):
    scale_key, value_key = jax.random.split(key)
    head_scale = jnp.exp(jax.random.uniform(scale_key, (HEADS, 1), jnp.float32, jnp.log(lowest), jnp.log(highest)))
    values = jax.random.normal(value_key, (HEADS, HEAD), jnp.float32) * head_scale
    return values.reshape(D).astype(jnp.bfloat16)


def draw_agg_query(key, part):
    key = jax.random.fold_in(key, 37)
    return query_values(key, 0.5, 2.0)


def shard_levels(own_key, extent, cuts, low, largest):
    loudness = 1.0
    for axis_at, blocks in cuts:
        draws = jax.random.uniform(jax.random.fold_in(jax.random.fold_in(own_key, 6), axis_at), (blocks,), jnp.float32, low / len(cuts), largest / len(cuts))
        loudness = loudness * jnp.repeat(jnp.exp(draws), extent[axis_at] // blocks).reshape((-1,) + (1,) * (len(extent) - 1 - axis_at))
    return loudness


def noise(key, dims, width, limit, pieces=(), kind=jnp.bfloat16):
    array = width * jax.random.normal(key, dims, jnp.float32)
    if pieces:
        array = array * shard_levels(key, dims, pieces, -0.22, 0.18)
    return jnp.clip(array, -limit, limit).astype(kind)


def setup_inputs(seed: int = 0) -> dict:
    seeds = jax.random.split(jax.random.key(seed), 12)
    pixels = noise(seeds[0], (SAMPLES, PATCHES, VMAX * PP), 1.0, 6.0, ((1, 256),))
    counts = draw_counts(jax.random.fold_in(seeds[11], 71), 0)
    var_ids = draw_var_ids(jax.random.fold_in(seeds[11], 71), 0)
    destination = jax.random.permutation(seeds[3], SAMPLES).astype(jnp.int32)
    embed_weight = noise(seeds[4], (NVAR, PP, D), PP ** -0.5, 1.5, ((2, 8),))
    var_embed = noise(seeds[5], (NVAR, D), 0.7, 4.0, ((1, 8),))
    agg_query = draw_agg_query(jax.random.fold_in(seeds[11], 71), 0)
    ln_gain = jnp.clip(1.0 + 0.15 * jax.random.normal(seeds[7], (1, D), jnp.float32), 0.25, 1.75).astype(jnp.bfloat16)
    fc_up = noise(seeds[8], (D, FF), D ** -0.5, 0.09375, ((1, 8),))
    fc_down = noise(seeds[9], (D, FF), FF ** -0.5, 0.0625, ((0, 32), (1, 8)))
    cotangent = noise(seeds[10], (SAMPLES, PATCHES, D), 1.0, 6.0, ((0, 32), (2, 8)))
    return dict(pixels=pixels, counts=counts, var_ids=var_ids, destination=destination, embed_weight=embed_weight, var_embed=var_embed, agg_query=agg_query, ln_gain=ln_gain, fc_up=fc_up, fc_down=fc_down, cotangent=cotangent)


def sample_pass(pixel_block, live_count, slot_ids, grad_out, embed_weight, var_embed, agg_query, ln_gain, fc_up, fc_down):
    score_scale = HEAD ** (-0.5)
    pix_slots = pixel_block.reshape(PATCHES, VMAX, PP)
    slot_weights = embed_weight[slot_ids].astype(jnp.float32)
    slot_bias = var_embed[slot_ids].astype(jnp.float32)
    embedded = (jnp.einsum('pjk,jkd->pjd', pix_slots.astype(jnp.float32), slot_weights) + slot_bias[None]).astype(jnp.bfloat16)
    by_head = embedded.reshape(PATCHES, VMAX, HEADS, HEAD).astype(jnp.float32)
    query = agg_query.reshape(HEADS, HEAD).astype(jnp.float32)
    scores = jnp.einsum('pjhc,hc->pjh', by_head, query) * score_scale
    live_mask = (jnp.arange(VMAX) < live_count)[None, :, None]
    scores = jnp.where(live_mask, scores, -jnp.inf)
    row_max = lax.optimization_barrier(jnp.max(scores, axis=1, keepdims=True))
    raised = jnp.exp(scores - row_max)
    attn_weights = raised / lax.optimization_barrier(jnp.sum(raised, axis=1, keepdims=True))
    attn_bf16 = attn_weights.astype(jnp.bfloat16).astype(jnp.float32)
    aggregate = jnp.einsum('pjh,pjhc->phc', attn_bf16, by_head).reshape(PATCHES, D).astype(jnp.bfloat16)
    agg_float = aggregate.astype(jnp.float32)
    row_mean = lax.optimization_barrier(jnp.mean(agg_float, axis=1, keepdims=True))
    row_var = lax.optimization_barrier(jnp.mean((agg_float - row_mean) ** 2, axis=1, keepdims=True))
    inv_std = lax.rsqrt(row_var + 1e-05)
    x_hat = (agg_float - row_mean) * inv_std
    gain_float = ln_gain.astype(jnp.float32)
    normed = (x_hat * gain_float).astype(jnp.bfloat16)
    pre_act = jnp.dot(normed, fc_up, preferred_element_type=jnp.float32)
    hidden = jax.nn.gelu(pre_act).astype(jnp.bfloat16)
    branch = lax.dot_general(hidden, fc_down, (((1,), (1,)), ((), ())), preferred_element_type=jnp.float32)
    mixed = (agg_float + branch).astype(jnp.bfloat16)
    grad_hidden = jnp.dot(grad_out, fc_down, preferred_element_type=jnp.float32)
    grad_pre = jax.vjp(jax.nn.gelu, pre_act)[1](grad_hidden)[0].astype(jnp.bfloat16)
    grad_normed = lax.dot_general(grad_pre, fc_up, (((1,), (1,)), ((), ())), preferred_element_type=jnp.float32)
    grad_std = grad_normed * gain_float
    plain_mean = lax.optimization_barrier(jnp.mean(grad_std, axis=1, keepdims=True))
    cross_mean = lax.optimization_barrier(jnp.mean(grad_std * x_hat, axis=1, keepdims=True))
    grad_agg = grad_out.astype(jnp.float32) + inv_std * (grad_std - plain_mean - x_hat * cross_mean)
    grad_agg_b = grad_agg.astype(jnp.bfloat16).astype(jnp.float32).reshape(PATCHES, HEADS, HEAD)
    grad_attn = jnp.einsum('phc,pjhc->pjh', grad_agg_b, by_head)
    grad_score = attn_weights * (grad_attn - lax.optimization_barrier(jnp.sum(attn_weights * grad_attn, axis=1, keepdims=True)))
    grad_emb = attn_weights[..., None] * grad_agg.reshape(PATCHES, 1, HEADS, HEAD) + grad_score[..., None] * query[None, None] * score_scale
    grad_emb = grad_emb.reshape(PATCHES, VMAX, D).astype(jnp.bfloat16).astype(jnp.float32)
    grad_score_b = grad_score.astype(jnp.bfloat16).astype(jnp.float32)
    grad_query = (jnp.einsum('pjh,pjhc->hc', grad_score_b, by_head) * score_scale).reshape(D)
    slot_grads = jnp.einsum('pjk,pjd->jkd', pix_slots.astype(jnp.float32), grad_emb)
    slot_bias_grads = lax.optimization_barrier(jnp.sum(grad_emb, axis=0))
    one_hot = ((slot_ids[:, None] == jnp.arange(NVAR)[None, :]) & (jnp.arange(VMAX) < live_count)[:, None]).astype(jnp.float32)
    table_embed = jnp.einsum('jv,jkd->vkd', one_hot, slot_grads, precision=lax.Precision.HIGHEST)
    table_var = jnp.dot(one_hot.T, slot_bias_grads, precision=lax.Precision.HIGHEST)
    return (mixed, table_embed, table_var, grad_query)

def reference(pixels, counts, var_ids, destination, embed_weight, var_embed, agg_query, ln_gain, fc_up, fc_down, cotangent):
    inverse = jnp.argsort(destination).astype(jnp.int32)

    def per_rank(totals, rank_here):
        sample = inverse[rank_here]
        mixed, table_embed, table_var, grad_query = sample_pass(pixels[sample], counts[sample], var_ids[sample], cotangent[rank_here], embed_weight, var_embed, agg_query, ln_gain, fc_up, fc_down)
        return ((totals[0] + table_embed, totals[1] + table_var, totals[2] + grad_query), mixed)
    start_totals = (jnp.zeros((NVAR, PP, D), jnp.float32), jnp.zeros((NVAR, D), jnp.float32), jnp.zeros((D,), jnp.float32))
    totals, mixed_all = lax.scan(per_rank, start_totals, jnp.arange(N_DP).astype(jnp.int32))
    return (mixed_all, totals[0], totals[1], totals[2])
```

```python
import functools

import jax
import jax.numpy as jnp
from jax import lax
from jax.experimental import pallas as pl
from jax.experimental.pallas import tpu as pltpu
from jax.sharding import Mesh, PartitionSpec as P

HEAD = 128
VMAX = 8
PP = 16
NVAR = 48
D = 4096
FF = 8192
NP = 256
W = 512
HID = 1024
EXT = NP + 16
BF = jnp.bfloat16
F32 = jnp.float32
NT = (((1,), (1,)), ((), ()))
VM = pl.BlockSpec(memory_space=pltpu.VMEM)
SM = pl.BlockSpec(memory_space=pltpu.SMEM)
NX, NY, NZ, NC = 4, 4, 8, 2


def params(mib):
    return pltpu.CompilerParams(vmem_limit_bytes=mib << 20)


def call(kernel, outs, n_smem, n_vmem, scratch=(), mib=24, flops=0, nbytes=0, name=None):
    single = not isinstance(outs, (list, tuple))
    return pl.pallas_call(
        kernel,
        out_shape=outs if single else tuple(outs),
        in_specs=[SM] * n_smem + [VM] * n_vmem,
        out_specs=VM if single else tuple([VM] * len(outs)),
        scratch_shapes=list(scratch),
        compiler_params=params(mib),
        cost_estimate=pl.CostEstimate(flops=flops, bytes_accessed=nbytes, transcendentals=0),
        name=name,
    )


def sds(shape, dtype):
    return jax.ShapeDtypeStruct(shape, dtype)


def send(a, axis, k):
    n = {"x": NX, "y": NY, "z": NZ, "c": NC}[axis]
    return lax.ppermute(a, axis, [(i, (i + k) % n) for i in range(n)])


def dot(a, b, dims=(((1,), (0,)), ((), ()))):
    return lax.dot_general(a, b, dims, preferred_element_type=F32)


def lane_group(shape):
    return lax.broadcasted_iota(jnp.int32, shape, 1) // 16


def head_mask(dtype):
    row = lax.broadcasted_iota(jnp.int32, (128, W), 0)
    col = lax.broadcasted_iota(jnp.int32, (128, W), 1)
    return jnp.where(row % 16 == col // HEAD, 1.0, 0.0).astype(dtype)


def over_slots(op, a):
    for shift in (16, 32, 64):
        a = op(a, pltpu.roll(a, shift, 1))
    return a


def fwd_kernel(ids, info, x_ref, onehot_ref, ew_ref, ve_ref, q_ref, gain_ref,
               agg_ref, emb_ref, attn_ref, wblk, wsem):
    copies = []
    for j in range(VMAX):
        copies.append(pltpu.make_async_copy(ew_ref.at[ids[j]], wblk.at[j, pl.ds(16 * j, 16), :], wsem.at[j]))
    zero = jnp.zeros((16, W), BF)
    for j in range(VMAX):
        for k in range(VMAX):
            if k != j:
                wblk[j, 16 * k:16 * (k + 1), :] = zero
    for cp in copies:
        cp.start()
    count = info[4]
    bias = dot(onehot_ref[...], ve_ref[...])
    expand = head_mask(BF)
    qmat = (expand.astype(F32) * q_ref[...].astype(F32)).astype(BF)
    for cp in copies:
        cp.wait()
    rows = 128
    group = lane_group((rows, 128))
    for r in range(NP // rows):
        at = slice(r * rows, (r + 1) * rows)
        x = x_ref[at, :]
        scores = jnp.zeros((rows, 128), F32)
        for j in range(VMAX):
            e = (dot(x, wblk[j]) + bias[j:j + 1, :]).astype(BF)
            emb_ref[j, at, :] = e
            scores = jnp.where(group == j, dot(e, qmat, NT), scores)
        scores = scores * (HEAD ** -0.5)
        scores = jnp.where(group < count, scores, -jnp.inf)
        top = over_slots(jnp.maximum, scores)
        raised = jnp.exp(scores - top)
        attn = raised / over_slots(jnp.add, raised)
        attn_ref[at, :] = attn
        attn_b = attn.astype(BF)
        total = jnp.zeros((rows, W), F32)
        for j in range(VMAX):
            wide = dot(jnp.where(group == j, attn_b, jnp.zeros_like(attn_b)), expand)
            total = total + wide * emb_ref[j, at, :].astype(F32)
        agg_ref[at, :] = total.astype(BF)
    agg_ref[NP:EXT, :] = jnp.broadcast_to(gain_ref[...], (16, W))


def attention_forward(ids, info, x, onehot, ew, ve, q, gain):
    return pl.pallas_call(
        fwd_kernel,
        out_shape=(sds((EXT, W), BF), sds((VMAX, NP, W), BF), sds((NP, 128), F32)),
        in_specs=[SM, SM, VM, VM, pl.BlockSpec(memory_space=pl.ANY), VM, VM, VM],
        out_specs=(VM, VM, VM),
        scratch_shapes=[pltpu.VMEM((VMAX, 128, W), BF), pltpu.SemaphoreType.DMA((VMAX,))],
        compiler_params=params(24),
        cost_estimate=pl.CostEstimate(flops=2 * 3 * 8 * 256 * 128 * 512, bytes_accessed=4 << 20, transcendentals=0),
        name="attn_fwd",
    )(ids, info, x, onehot, ew, ve, q, gain)


def x_gather(a, half):
    left, right = send(a, "x", 1), send(a, "x", -1)
    return a, left, right, send(left[:half], "x", 1), send(right[half:], "x", -1)


def tensor_gather(a, half=128):
    mine = x_gather(a, half)
    return mine + tuple(send(p, "c", 1) for p in mine)


def blocks_of(info, refs):
    x, c = info[2], info[3]
    out = []
    for k, core in ((0, c), (1, 1 - c)):
        own, left, right, opp_a, opp_b = refs[5 * k:5 * k + 5]
        out.append((2 * x + core, (own,)))
        out.append((2 * ((x + 3) % 4) + core, (left,)))
        out.append((2 * ((x + 1) % 4) + core, (right,)))
        out.append((2 * ((x + 2) % 4) + core, (opp_a, opp_b)))
    return out


def part(refs, lo, hi):
    if len(refs) == 1:
        return refs[0][lo:hi, :]
    return refs[0][lo:hi, :] if hi <= 128 else refs[1][lo - 128:hi - 128, :]


def up_kernel(info, *refs):
    pieces, up_ref = refs[:10], refs[10]
    pre_ref, dg_ref, hid_ref, u_ref, st_ref, nrm = refs[11:]

    @pl.when(pl.program_id(0) == 0)
    def _():
        blocks = blocks_of(info, pieces)
        for r in range(4):
            lo, hi = 64 * r, 64 * r + 64
            total = jnp.zeros((64, W), F32)
            for _, p in blocks:
                total = total + part(p, lo, hi).astype(F32)
            mean = jnp.sum(total, axis=1, keepdims=True) * (1.0 / D)
            total = jnp.zeros((64, W), F32)
            for _, p in blocks:
                d = part(p, lo, hi).astype(F32) - mean
                total = total + d * d
            inv = lax.rsqrt(jnp.sum(total, axis=1, keepdims=True) * (1.0 / D) + 1e-05)
            st_ref[0, lo:hi, :] = jnp.broadcast_to(mean, (64, 128))
            st_ref[1, lo:hi, :] = jnp.broadcast_to(inv, (64, 128))
            for b, p in blocks:
                gain = part(p, NP, EXT)[0:1, :].astype(F32)
                col = pl.ds(pl.multiple_of(b * W, W), W)
                nrm[lo:hi, col] = ((part(p, lo, hi).astype(F32) - mean) * inv * gain).astype(BF)
        for b, p in blocks:
            nrm[NP:EXT, pl.ds(pl.multiple_of(b * W, W), W)] = part(p, NP, EXT)

    acc = dot(nrm[...], up_ref[...])
    x = acc[:NP]
    c = 0.7978845608028654
    th = jnp.tanh(c * (x + 0.044715 * (x * x * x)))
    pre_ref[...] = x
    hid_ref[...] = (0.5 * x * (1.0 + th)).astype(BF)
    dg_ref[...] = 0.5 * (1.0 + th) + 0.5 * x * (1.0 - th * th) * (c * (1.0 + 3 * 0.044715 * (x * x)))
    u_ref[...] = acc[NP:NP + 8]


def up_call(info, pieces, fc_up):
    n = 4
    w = HID // n
    whole = [pl.BlockSpec(p.shape, lambda i: (0, 0)) for p in pieces]
    return pl.pallas_call(
        up_kernel,
        grid=(n,),
        out_shape=(sds((NP, HID), F32), sds((NP, HID), F32), sds((NP, HID), BF), sds((8, HID), F32), sds((2, NP, 128), F32)),
        in_specs=[SM] + whole + [pl.BlockSpec((D, w), lambda i: (0, i))],
        out_specs=(
            pl.BlockSpec((NP, w), lambda i: (0, i)), pl.BlockSpec((NP, w), lambda i: (0, i)),
            pl.BlockSpec((NP, w), lambda i: (0, i)), pl.BlockSpec((8, w), lambda i: (0, i)),
            pl.BlockSpec((2, NP, 128), lambda i: (0, 0, 0)),
        ),
        scratch_shapes=[pltpu.VMEM((EXT, D), BF)],
        compiler_params=params(32),
        cost_estimate=pl.CostEstimate(flops=2 * EXT * D * HID, bytes_accessed=16 << 20, transcendentals=0),
        name="ln_up",
    )(info, *pieces, fc_up)


def split3(row):
    hi = row.astype(BF).astype(F32)
    mid = (row - hi).astype(BF).astype(F32)
    return hi, mid, row - hi - mid


def ride(row):
    hi, mid, low = split3(row)
    at = lax.broadcasted_iota(jnp.int32, (16, W), 0)
    tile = jnp.where(at == 0, hi, jnp.where(at == 1, mid, jnp.where(at == 2, low, 0.0)))
    return tile.astype(BF)


def unride(tile):
    return jnp.sum(tile.astype(F32), axis=0, keepdims=True)


def gh_kernel(info, *refs):
    pieces, down_ref, pre_ref, dg_ref, u_ref = refs[:10], refs[10], refs[11], refs[12], refs[13]
    gp_ref, s_ref, g, tot = refs[14:]
    i = pl.program_id(0)

    @pl.when(i == 0)
    def _():
        for b, p in blocks_of(info, pieces):
            col = pl.ds(pl.multiple_of(b * W, W), W)
            for lo in (0, 128):
                g[lo:lo + 128, col] = part(p, lo, lo + 128)
        tot[...] = jnp.zeros_like(tot)

    gh = dot(g[...], down_ref[...])
    gp = (gh * dg_ref[...]).astype(BF)
    gp_ref[...] = gp
    gpf = gp.astype(F32)
    a = gpf * u_ref[0:1, :]
    b = gpf * pre_ref[...]
    tot[0] += a[:, :128] + a[:, 128:]
    tot[1] += b[:, :128] + b[:, 128:]

    @pl.when(i == pl.num_programs(0) - 1)
    def _():
        s_ref[...] = ride(sums_row(tot[0], tot[1]))


def sums_row(a, b):
    rows = []
    for t in (a, b):
        s = jnp.broadcast_to(jnp.sum(t, axis=1, keepdims=True), (NP, 128))
        rows.append(jnp.transpose(s)[0:1, :])
    return jnp.concatenate(rows, axis=1)


def gh_call(info, pieces, down, pre, dg, u):
    n = 4
    w = HID // n
    whole = [pl.BlockSpec(p.shape, lambda i: (0, 0)) for p in pieces]
    col = lambda r: pl.BlockSpec((r, w), lambda i: (0, i))
    return pl.pallas_call(
        gh_kernel,
        grid=(n,),
        out_shape=(sds((NP, HID), BF), sds((16, W), BF)),
        in_specs=[SM] + whole + [col(D), col(NP), col(NP), col(8)],
        out_specs=(col(NP), pl.BlockSpec((16, W), lambda i: (0, 0))),
        scratch_shapes=[pltpu.VMEM((NP, D), BF), pltpu.VMEM((2, NP, 128), F32)],
        compiler_params=params(32),
        cost_estimate=pl.CostEstimate(flops=2 * NP * D * HID, bytes_accessed=12 << 20, transcendentals=0),
        name="grad_hidden",
    )(info, *pieces, down, pre, dg, u)


def nt_kernel(with_sums, with_add, order, *refs):
    tab, lhs_ref, rhs_ref = refs[:3]
    rest = list(refs[3:])
    s_ref = rest.pop(0) if with_sums else None
    add_ref = rest.pop(0) if with_add else None
    out_ref = rest.pop(0)
    acc = dot(lhs_ref[...], rhs_ref[...], NT)
    if with_add:
        acc = acc + add_ref[0, :NP, :].astype(F32)
    out_ref[0, :NP, :] = acc.astype(BF)
    if with_sums:
        if with_add:
            out_ref[0, NP:, :] = ride(unride(s_ref[...]) + unride(add_ref[0, NP:, :]))
        else:
            out_ref[0, NP:, :] = s_ref[...]


def nt_call(tab, lhs, rhs, sums=None, add=None, add_at=None, n=4, name=None):
    rows = EXT if sums is not None else NP
    in_specs = [
        pl.BlockSpec((NP, HID), lambda i, t: (0, 0)),
        pl.BlockSpec((W, HID), lambda i, t: (t[i], 0)),
    ]
    args = [lhs, rhs]
    if sums is not None:
        in_specs.append(pl.BlockSpec((16, W), lambda i, t: (0, 0)))
        args.append(sums)
    if add is not None:
        at = add_at
        in_specs.append(pl.BlockSpec((1, rows, W), lambda i, t: (i + at, 0, 0)))
        args.append(add)
    return pl.pallas_call(
        functools.partial(nt_kernel, sums is not None, add is not None, None),
        grid_spec=pltpu.PrefetchScalarGridSpec(
            num_scalar_prefetch=1,
            grid=(n,),
            in_specs=in_specs,
            out_specs=pl.BlockSpec((1, rows, W), lambda i, t: (i, 0, 0)),
        ),
        out_shape=sds((n, rows, W), BF),
        compiler_params=params(24),
        cost_estimate=pl.CostEstimate(flops=2 * NP * HID * W * n, bytes_accessed=n << 20, transcendentals=0),
        name=name,
    )(tab, *args)


def add_kernel(with_sums, a_ref, b_ref, out_ref):
    n = a_ref.shape[0]
    m = n - 16 if with_sums else n
    out_ref[:m, :] = (a_ref[:m, :].astype(F32) + b_ref[:m, :].astype(F32)).astype(BF)
    if with_sums:
        out_ref[m:, :] = ride(unride(a_ref[m:, :]) + unride(b_ref[m:, :]))


def add(a, b, with_sums=False):
    return call(functools.partial(add_kernel, with_sums), sds(a.shape, BF), 0, 2, nbytes=1 << 20, name="add")(a, b)


def tensor_scatter(info, lhs, rhs, sums, name):
    x, c = info[2], info[3]
    chips = [(x + k) % 4 for k in (2, 1, 3, 0)]
    other = jnp.stack([2 * k + 1 - c for k in chips])
    mine = jnp.stack([2 * k + c for k in chips])
    o = nt_call(other, lhs, rhs, sums, name=name + "_o")
    o = send(o, "c", 1)
    far = nt_call(mine[:1], lhs, rhs, sums, o, 0, n=1, name=name + "_f")[0]
    got_a, got_b = send(far[:128], "x", 1), send(far[128:], "x", -1)
    near = nt_call(mine[1:], lhs, rhs, sums, o, 1, n=3, name=name + "_n")
    right, left, own = near[0], near[1], near[2]
    right, left = merge_call(right, left, got_a, got_b, sums is not None)
    return own, send(right, "x", 1), send(left, "x", -1)


def merge_kernel(with_sums, r_ref, l_ref, a_ref, b_ref, ro, lo):
    ro[:128, :] = (r_ref[:128, :].astype(F32) + a_ref[...].astype(F32)).astype(BF)
    ro[128:, :] = r_ref[128:, :]
    lo[:128, :] = l_ref[:128, :]
    lo[128:NP, :] = (l_ref[128:NP, :].astype(F32) + b_ref[:128, :].astype(F32)).astype(BF)
    if with_sums:
        lo[NP:, :] = ride(unride(l_ref[NP:, :]) + unride(b_ref[128:, :]))


def merge_call(r, l, a, b, with_sums):
    return call(functools.partial(merge_kernel, with_sums), (sds(r.shape, BF), sds(l.shape, BF)), 0, 4,
                nbytes=1 << 20, name="merge")(r, l, a, b)


def bwd_kernel(info, own_ref, p1_ref, p2_ref, agg_ref, st_ref, gain_ref, g_ref, emb_ref, attn_ref, x_ref, q_ref,
               *rest):
    outs, acc = rest[:4], rest[4]
    expand = head_mask(BF)
    scale = HEAD ** -0.5
    qrow = q_ref[...].astype(F32) * scale
    gain = gain_ref[...].astype(F32)
    sums = unride(own_ref[NP:, :]) + unride(p1_ref[NP:, :]) + unride(p2_ref[NP:, :])
    cols = []
    for k in range(2):
        row = sums[:, k * NP:(k + 1) * NP] * (1.0 / D)
        cols.append(jnp.transpose(jnp.broadcast_to(row, (128, NP))))
    expand2 = jnp.concatenate([expand, expand], axis=0)
    rows = 128
    group = lane_group((rows, 128))
    group2 = lax.broadcasted_iota(jnp.int32, (rows, 256), 1) % 128 // 16
    gq = jnp.zeros((8, W), F32)
    for r in range(NP // rows):
        at = slice(r * rows, (r + 1) * rows)
        mean, inv = st_ref[0, at, 0:1], st_ref[1, at, 0:1]
        xh = (agg_ref[at, :].astype(F32) - mean) * inv
        gs = (own_ref[at, :].astype(F32) + p1_ref[at, :].astype(F32) + p2_ref[at, :].astype(F32)) * gain
        ga = g_ref[at, :].astype(F32) + inv * (gs - cols[0][at, 0:1] - xh * cols[1][at, 0:1])
        gab = ga.astype(BF).astype(F32)
        gattn = jnp.zeros((rows, 128), F32)
        for j in range(VMAX):
            prod = gab * emb_ref[j, at, :].astype(F32)
            hi = prod.astype(BF)
            low = (prod - hi.astype(F32)).astype(BF)
            both = dot(hi, expand, NT) + dot(low, expand, NT)
            gattn = jnp.where(group == j, both, gattn)
        attn = attn_ref[at, :]
        gscore = attn * (gattn - over_slots(jnp.add, attn * gattn))
        ahi = attn.astype(BF)
        alow = (attn - ahi.astype(F32)).astype(BF)
        shi = gscore.astype(BF)
        slow = (gscore - shi.astype(F32)).astype(BF)
        a2 = jnp.concatenate([ahi, alow], axis=1)
        s2 = jnp.concatenate([shi, slow], axis=1)
        zero = jnp.zeros_like(a2)
        xt = jnp.transpose(x_ref[at, :].astype(F32)).astype(BF)
        ones = jnp.ones((16, rows), BF)
        for j in range(VMAX):
            pick = group2 == j
            a_w = dot(jnp.where(pick, a2, zero), expand2)
            s_w = dot(jnp.where(pick, s2, zero), expand2)
            ge = (a_w * ga + s_w * qrow).astype(BF)
            e = emb_ref[j, at, :].astype(F32)
            part_q = s_w.astype(BF).astype(F32) * e
            for k in range(rows // 8):
                gq = gq + part_q[8 * k:8 * k + 8, :]
            lhs = jnp.concatenate([xt[16 * j:16 * j + 16, :], ones], axis=0)
            got = dot(lhs, ge)
            if r == 0:
                acc[16 * j:16 * j + 16, :] = got[:16]
                acc[128 + j:129 + j, :] = got[16:17]
            else:
                acc[16 * j:16 * j + 16, :] += got[:16]
                acc[128 + j:129 + j, :] += got[16:17]
    acc[136:137, :] = jnp.sum(gq, axis=0, keepdims=True) * scale
    acc[137:144, :] = jnp.zeros((7, W), F32)
    for k, out in enumerate(outs):
        col = pl.multiple_of((info[0] + k) % NY * 128, 128)
        out[...] = acc[:, pl.ds(col, 128)].astype(BF)


def attention_backward(info, gn, agg, st, gain, g, emb, attn, x, q):
    return call(
        bwd_kernel, [sds((144, 128), BF)] * 4, 1, 11, [pltpu.VMEM((144, W), F32)], mib=24,
        flops=2 * 6 * 8 * 256 * 128 * 512, nbytes=5 << 20, name="attn_bwd",
    )(info, *gn, agg, st, gain, g, emb, attn, x, q)


def sum_kernel(info, ids, counts, onehot_ref, *refs):
    pieces, out_ref, acc, bias, query = refs[:9], refs[9], refs[10], refs[11], refs[12]
    acc[...] = jnp.zeros_like(acc)
    query[...] = jnp.zeros_like(query)
    y, z = info[0], info[1]
    for zk in range(NZ):
        zr = (z + zk) % NZ
        for yk in range(NY):
            yr = (y + (0, 3, 1, 2)[yk]) % NY
            rank = yr * NZ + zr
            if zk == 4:
                ref, base = (pieces[4], 144 * yk) if yk < 2 else (pieces[5], 144 * (yk - 2))
            else:
                ref, base = pieces[zk if zk < 4 else zk + 1], 144 * yk
            data = ref[base:base + 144, :].astype(F32)
            live = counts[rank]
            for j in range(VMAX):
                v = ids[rank * VMAX + j]

                @pl.when(j < live)
                def _():
                    acc[v] += data[16 * j:16 * j + 16]
            row = pl.multiple_of(rank * VMAX, VMAX)
            bias[pl.ds(row, VMAX), :] = data[128:136]
            query[...] += data[136:144]
    for v in range(NVAR):
        out_ref[16 * v:16 * v + 16, :] = acc[v].astype(BF)
    b = bias[...]
    hi = b.astype(BF)
    out_ref[768:816, :] = dot(onehot_ref[...], hi).astype(BF)
    at = lax.broadcasted_iota(jnp.int32, (16, 128), 0)
    out_ref[816:832, :] = jnp.where(at == 0, query[0:1, :], 0.0).astype(BF)


def out_kernel(info, own, left, right, opp_a, opp_b, ge_ref, gv_ref, gq_ref):
    y = info[0]
    for k, refs in ((0, (own,)), (3, (left,)), (1, (right,)), (2, (opp_a, opp_b))):
        col = pl.ds(pl.multiple_of((y + k) % NY * 128, 128), 128)
        first = refs[0]
        for v in range(NVAR):
            src = first[16 * v:16 * v + 16, :] if (len(refs) == 1 or v < 26) else refs[1][16 * (v - 26):16 * (v - 26) + 16, :]
            ge_ref[v, :, col] = src.astype(F32)
        tail = refs[-1]
        base = 768 if len(refs) == 1 else 768 - 416
        gv_ref[:, col] = tail[base:base + 48, :].astype(F32)
        gq_ref[:, col] = tail[base + 48:base + 64, :].astype(F32)[0:8]


def gradient_exchange(info, ids_by_rank, counts_by_rank, onehot, outs):
    own, p1, p2, p3 = outs
    block = jnp.concatenate([own, send(p1, "y", 1), send(p3, "y", -1), send(p2, "y", 2)], axis=0)
    up = [block]
    down = [block]
    for _ in range(3):
        up.append(send(up[-1], "z", 1))
        down.append(send(down[-1], "z", -1))
    far_a = send(up[3][:288], "z", 1)
    far_b = send(down[3][288:], "z", -1)
    pieces = [block, down[1], down[2], down[3], far_a, far_b, up[3], up[2], up[1]]
    dense = call(
        sum_kernel, sds((832, 128), BF), 3, 10,
        [pltpu.VMEM((NVAR, PP, 128), F32), pltpu.VMEM((256, 128), F32), pltpu.VMEM((8, 128), F32)],
        mib=16, flops=1 << 20, nbytes=2 << 20, name="slot_sum",
    )(info, ids_by_rank, counts_by_rank, onehot, *pieces)
    left, right = send(dense, "y", 1), send(dense, "y", -1)
    opp_a, opp_b = send(left[:416], "y", 1), send(right[416:], "y", -1)
    return call(
        out_kernel, (sds((NVAR, PP, W), F32), sds((NVAR, W), F32), sds((8, W), F32)), 1, 5,
        mib=16, flops=1 << 20, nbytes=3 << 20, name="spread",
    )(info, dense, left, right, opp_a, opp_b)


def mix_kernel(agg_ref, own, p1, p2, out_ref):
    s = own[...].astype(F32) + p1[...].astype(F32) + p2[...].astype(F32)
    out_ref[0] = (agg_ref[:NP, :].astype(F32) + s).astype(BF)


def local(pixels, counts, var_ids, destination, embed_weight, var_embed, agg_query, ln_gain, fc_up, fc_down, cotangent):
    y, z, x, c = (lax.axis_index(a) for a in ("y", "z", "x", "c"))
    rank = y * NZ + z
    to_rank = destination[None, :] == jnp.arange(NY * NZ)[:, None]
    ordered = dot(to_rank.astype(BF), pixels[:, 0, :]).astype(BF)
    picked = to_rank.astype(jnp.int32)
    counts_by_rank = jnp.sum(picked * counts[None, :], axis=1)
    ids_by_rank = jnp.sum(picked[:, :, None] * var_ids[None], axis=1)
    live = jnp.arange(VMAX)[None, :] < counts_by_rank[:, None]
    onehot = (
        (ids_by_rank.reshape(1, -1) == jnp.arange(NVAR)[:, None]) & live.reshape(1, -1)
    ).astype(BF)
    ids = lax.dynamic_slice(ids_by_rank, (rank, 0), (1, VMAX))[0]
    count = lax.dynamic_slice(counts_by_rank, (rank,), (1,))[0]
    info = jnp.stack([y, z, x, c, count]).astype(jnp.int32)
    slot_onehot = (jnp.pad(ids, (0, 8), constant_values=-1)[:, None] == jnp.arange(NVAR)[None, :]).astype(BF)

    down = lax.all_gather(fc_down, ("y", "z"), axis=0, tiled=True)

    mine = lax.all_to_all(ordered, ("y", "z"), 0, 0, tiled=True)
    mine = lax.all_gather(mine.reshape(NY * NZ, 1, 128), ("x", "c"), axis=1, tiled=True).reshape(NP, 128)

    q = agg_query.reshape(1, W)
    agg, emb, attn = attention_forward(ids, info, mine, slot_onehot, embed_weight, var_embed, q, ln_gain)
    g_own = cotangent[0]
    g_pieces = tensor_gather(g_own)
    pieces = tensor_gather(agg)
    pre, dg, hid, u, st = up_call(info, pieces, fc_up)
    gp, sums = gh_call(info, g_pieces, down, pre, dg, u)
    gn = tensor_scatter(info, gp, fc_up, sums, "gn")
    outs = attention_backward(info, gn, agg, st, ln_gain, g_own, emb, attn, mine, q)
    br = tensor_scatter(info, hid, down, None, "br")
    mixed = call(mix_kernel, sds((1, NP, W), BF), 0, 4, nbytes=1 << 20, name="mix")(agg, *br)
    ge, gv, gq = gradient_exchange(info, ids_by_rank.reshape(-1), counts_by_rank, onehot, outs)
    return mixed, ge, gv, gq[0]


def solution(mesh):
    fine = Mesh(mesh.devices.reshape(NY, NZ, NX, NC), ("y", "z", "x", "c"))
    dp, tensor = ("y", "z"), ("x", "c")
    in_specs = (
        P(None, dp + tensor, None), P(), P(), P(), P(None, None, tensor), P(None, tensor), P(tensor),
        P(None, tensor), P(None, tensor), P(dp, tensor), P(dp, None, tensor),
    )
    out_specs = (P(dp, None, tensor), P(None, None, tensor), P(None, tensor), P(tensor))
    return jax.shard_map(local, mesh=fine, in_specs=in_specs, out_specs=out_specs, check_vma=False)
```

```python
import functools

import jax
import jax.numpy as jnp
from jax import lax
from jax.experimental import pallas as pl
from jax.experimental.pallas import tpu as pltpu
from jax.sharding import Mesh, PartitionSpec as P

HEAD = 128
VMAX = 8
PP = 16
NVAR = 48
D = 4096
FF = 8192
NP = 256
W = 512
HID = 1024
EXT = NP + 16
BF = jnp.bfloat16
F32 = jnp.float32
NT = (((1,), (1,)), ((), ()))
VM = pl.BlockSpec(memory_space=pltpu.VMEM)
SM = pl.BlockSpec(memory_space=pltpu.SMEM)
NX, NY, NZ, NC = 4, 4, 8, 2
BIG = 16


def params(mib):
    return pltpu.CompilerParams(vmem_limit_bytes=mib << 20)


def call(kernel, outs, n_smem, n_vmem, scratch=(), mib=BIG, flops=0, nbytes=0, name=None):
    single = not isinstance(outs, (list, tuple))
    return pl.pallas_call(
        kernel,
        out_shape=outs if single else tuple(outs),
        in_specs=[SM] * n_smem + [VM] * n_vmem,
        out_specs=VM if single else tuple([VM] * len(outs)),
        scratch_shapes=list(scratch),
        compiler_params=params(mib),
        cost_estimate=pl.CostEstimate(flops=flops, bytes_accessed=nbytes, transcendentals=0),
        name=name,
    )


def sds(shape, dtype):
    return jax.ShapeDtypeStruct(shape, dtype)


def hbm(a):
    return pltpu.with_memory_space_constraint(a, pltpu.HBM)


def send(a, axis, k):
    n = {"x": NX, "y": NY, "z": NZ, "c": NC}[axis]
    return lax.ppermute(a, axis, [(i, (i + k) % n) for i in range(n)])


def around(a, axis):
    n = {"x": NX, "y": NY, "z": NZ}[axis]
    steps = [(2 * i + k, 2 * ((i + 1 - 2 * k) % n) + k) for i in range(n) for k in range(NC)]
    return lax.ppermute(a, (axis, "c"), steps)


def dot(a, b, dims=(((1,), (0,)), ((), ()))):
    return lax.dot_general(a, b, dims, preferred_element_type=F32)


def lane_group(shape):
    return lax.broadcasted_iota(jnp.int32, shape, 1) // 16


def head_mask(dtype):
    row = lax.broadcasted_iota(jnp.int32, (128, W), 0)
    col = lax.broadcasted_iota(jnp.int32, (128, W), 1)
    return jnp.where(row % 16 == col // HEAD, 1.0, 0.0).astype(dtype)


def over_slots(op, a):
    for shift in (16, 32, 64):
        a = op(a, pltpu.roll(a, shift, 1))
    return a


def find(destination, rank):
    return lax.fori_loop(0, NY * NZ, lambda i, s: jnp.where(destination[i] == rank, i, s), 0)


def fwd_kernel(info, destination, counts, var_ids, xa_ref, xb_ref, ew_ref, ve_ref, q_ref, gain_ref,
               agg_ref, emb_ref, attn_ref, x_ref, wblk, wsem):
    copies = []
    sample = find(destination, info[0] * NZ + info[1])
    count = counts[sample]
    ids = [var_ids[sample * VMAX + j] for j in range(VMAX)]
    for j in range(VMAX):
        copies.append(pltpu.make_async_copy(ew_ref.at[ids[j]], wblk.at[j, pl.ds(16 * j, 16), :], wsem.at[j]))
    zero = jnp.zeros((16, W), BF)
    for j in range(VMAX):
        for k in range(VMAX):
            if k != j:
                wblk[j, 16 * k:16 * (k + 1), :] = zero
    for cp in copies:
        cp.start()
    col = lax.broadcasted_iota(jnp.int32, (1, NP), 1)
    device = jnp.zeros((1, NP), jnp.int32)
    for k in range(8):
        chip, core = (info[2] + (0, 3, 1, 2)[k % 4]) % 4, (info[3] + k // 4) % 2
        device = jnp.where(col // 32 == k, 2 * chip + core, device)
    row = lax.broadcasted_iota(jnp.int32, (NP, NP), 0)
    order = jnp.where(row == 8 * (col % 32) + device, 1.0, 0.0).astype(BF)
    pieces = jnp.concatenate([r[k] for r in (xa_ref, xb_ref) for k in range(4)], axis=0)
    x_ref[...] = dot(order, pieces).astype(BF)
    at_slot = lax.broadcasted_iota(jnp.int32, (16, NVAR), 0)
    at_var = lax.broadcasted_iota(jnp.int32, (16, NVAR), 1)
    onehot = jnp.zeros((16, NVAR), F32)
    for j in range(VMAX):
        onehot = jnp.where((at_slot == j) & (at_var == ids[j]), 1.0, onehot)
    bias = dot(onehot.astype(BF), ve_ref[...])
    expand = head_mask(BF)
    qmat = (expand.astype(F32) * q_ref[...].astype(F32)).astype(BF)
    for cp in copies:
        cp.wait()
    rows = 128
    group = lane_group((rows, 128))
    for r in range(NP // rows):
        at = slice(r * rows, (r + 1) * rows)
        x = x_ref[at, :]
        scores = jnp.zeros((rows, 128), F32)
        for j in range(VMAX):
            e = (dot(x, wblk[j]) + bias[j:j + 1, :]).astype(BF)
            emb_ref[j, at, :] = e
            scores = jnp.where(group == j, dot(e, qmat, NT), scores)
        scores = scores * (HEAD ** -0.5)
        scores = jnp.where(group < count, scores, -jnp.inf)
        top = over_slots(jnp.maximum, scores)
        raised = jnp.exp(scores - top)
        attn = raised / over_slots(jnp.add, raised)
        attn_ref[at, :] = attn
        attn_b = attn.astype(BF)
        total = jnp.zeros((rows, W), F32)
        for j in range(VMAX):
            wide = dot(jnp.where(group == j, attn_b, jnp.zeros_like(attn_b)), expand)
            total = total + wide * emb_ref[j, at, :].astype(F32)
        agg_ref[at, :] = total.astype(BF)
    agg_ref[NP:EXT, :] = jnp.broadcast_to(gain_ref[...], (16, W))


def attention_forward(info, routing, xs, ew, ve, q, gain):
    return pl.pallas_call(
        fwd_kernel,
        out_shape=(sds((EXT, W), BF), sds((VMAX, NP, W), BF), sds((NP, 128), F32), sds((NP, 128), BF)),
        in_specs=[SM] * 4 + [VM, VM, pl.BlockSpec(memory_space=pl.ANY), VM, VM, VM],
        out_specs=(VM, VM, VM, VM),
        scratch_shapes=[pltpu.VMEM((VMAX, 128, W), BF), pltpu.SemaphoreType.DMA((VMAX,))],
        compiler_params=params(BIG),
        cost_estimate=pl.CostEstimate(flops=2 * 3 * 8 * 256 * 128 * 512, bytes_accessed=4 << 20, transcendentals=0),
        name="attn_fwd",
    )(info, *routing, *xs, ew, ve, q, gain)


def tensor_gather(a):
    first = around(a, "x")
    other = send(a, "c", 1)
    second = around(other, "x")
    far = around(first, "x")
    return a, other, first, second, far, send(first, "c", 1), send(second, "c", 1), send(far, "c", 1)


def blocks_of(info, refs):
    x, c = info[2], info[3]
    d = 1 - 2 * c
    back, fore, opposite = (x + 4 - d) % 4, (x + 4 + d) % 4, (x + 2) % 4
    place = ((x, c), (x, 1 - c), (back, c), (back, 1 - c), (opposite, c), (fore, 1 - c), (fore, c), (opposite, 1 - c))
    return [(chip, core, ref) for (chip, core), ref in zip(place, refs)]


def up_kernel(info, *refs):
    pieces, up_ref = refs[:8], refs[8]
    pre_ref, dg_ref, hid_ref, u_ref, st_ref, nrm = refs[9:]

    @pl.when(pl.program_id(0) == 0)
    def _():
        blocks = [(2 * chip + core, p) for chip, core, p in blocks_of(info, pieces)]
        for r in range(4):
            lo, hi = 64 * r, 64 * r + 64
            total = jnp.zeros((64, W), F32)
            for _, p in blocks:
                total = total + p[lo:hi, :].astype(F32)
            mean = jnp.sum(total, axis=1, keepdims=True) * (1.0 / D)
            total = jnp.zeros((64, W), F32)
            for _, p in blocks:
                d = p[lo:hi, :].astype(F32) - mean
                total = total + d * d
            inv = lax.rsqrt(jnp.sum(total, axis=1, keepdims=True) * (1.0 / D) + 1e-05)
            st_ref[0, lo:hi, :] = jnp.broadcast_to(mean, (64, 128))
            st_ref[1, lo:hi, :] = jnp.broadcast_to(inv, (64, 128))
            for b, p in blocks:
                gain = p[NP:EXT, :][0:1, :].astype(F32)
                col = pl.ds(pl.multiple_of(b * W, W), W)
                nrm[lo:hi, col] = ((p[lo:hi, :].astype(F32) - mean) * inv * gain).astype(BF)
        for b, p in blocks:
            nrm[NP:EXT, pl.ds(pl.multiple_of(b * W, W), W)] = p[NP:EXT, :]

    acc = dot(nrm[...], up_ref[...])
    x = acc[:NP]
    c = 0.7978845608028654
    th = jnp.tanh(c * (x + 0.044715 * (x * x * x)))
    pre_ref[...] = x
    hid_ref[...] = (0.5 * x * (1.0 + th)).astype(BF)
    dg_ref[...] = 0.5 * (1.0 + th) + 0.5 * x * (1.0 - th * th) * (c * (1.0 + 3 * 0.044715 * (x * x)))
    u_ref[...] = acc[NP:NP + 8]


def up_call(info, pieces, fc_up):
    n = 4
    w = HID // n
    whole = [pl.BlockSpec(p.shape, lambda i: (0, 0)) for p in pieces]
    return pl.pallas_call(
        up_kernel,
        grid=(n,),
        out_shape=(sds((NP, HID), F32), sds((NP, HID), F32), sds((NP, HID), BF), sds((8, HID), F32), sds((2, NP, 128), F32)),
        in_specs=[SM] + whole + [pl.BlockSpec((D, w), lambda i: (0, i))],
        out_specs=(
            pl.BlockSpec((NP, w), lambda i: (0, i)), pl.BlockSpec((NP, w), lambda i: (0, i)),
            pl.BlockSpec((NP, w), lambda i: (0, i)), pl.BlockSpec((8, w), lambda i: (0, i)),
            pl.BlockSpec((2, NP, 128), lambda i: (0, 0, 0)),
        ),
        scratch_shapes=[pltpu.VMEM((EXT, D), BF)],
        compiler_params=params(BIG),
        cost_estimate=pl.CostEstimate(flops=2 * EXT * D * HID, bytes_accessed=16 << 20, transcendentals=0),
        name="ln_up",
    )(info, *map(hbm, pieces), hbm(fc_up))


def split3(row):
    hi = row.astype(BF).astype(F32)
    mid = (row - hi).astype(BF).astype(F32)
    return hi, mid, row - hi - mid


def ride(row):
    hi, mid, low = split3(row)
    at = lax.broadcasted_iota(jnp.int32, (16, W), 0)
    tile = jnp.where(at == 0, hi, jnp.where(at == 1, mid, jnp.where(at == 2, low, 0.0)))
    return tile.astype(BF)


def unride(tile):
    return jnp.sum(tile.astype(F32), axis=0, keepdims=True)


def join_kernel(info, *refs):
    pieces, out = refs[:8], refs[8]
    for chip, core, p in blocks_of(info, pieces):
        out[:, pl.ds(pl.multiple_of((2 * chip + core) * W, W), W)] = p[...]


def join(info, pieces):
    return call(join_kernel, sds((NP, D), BF), 1, 8, mib=BIG, nbytes=4 << 20, name="join")(info, *map(hbm, pieces))


def gh_kernel(g, down_ref, pre_ref, dg_ref, u_ref, gp_ref, s_ref, tot):
    i = pl.program_id(0)

    @pl.when(i == 0)
    def _():
        tot[...] = jnp.zeros_like(tot)

    gh = dot(g[...], down_ref[...])
    gp = (gh * dg_ref[...]).astype(BF)
    gp_ref[...] = gp
    gpf = gp.astype(F32)
    a = gpf * u_ref[0:1, :]
    b = gpf * pre_ref[...]
    tot[0] += a[:, :128] + a[:, 128:]
    tot[1] += b[:, :128] + b[:, 128:]

    @pl.when(i == pl.num_programs(0) - 1)
    def _():
        s_ref[...] = ride(sums_row(tot[0], tot[1]))


def grad_pre(g, down, pre, dg, u):
    n = 4
    w = HID // n

    def col(r):
        return pl.BlockSpec((r, w), lambda i: (0, i))

    return pl.pallas_call(
        gh_kernel,
        grid=(n,),
        out_shape=(sds((NP, HID), BF), sds((16, W), BF)),
        in_specs=[VM, col(D), col(NP), col(NP), col(8)],
        out_specs=(col(NP), pl.BlockSpec((16, W), lambda i: (0, 0))),
        scratch_shapes=[pltpu.VMEM((2, NP, 128), F32)],
        compiler_params=params(BIG),
        cost_estimate=pl.CostEstimate(flops=2 * NP * D * HID, bytes_accessed=12 << 20, transcendentals=0),
        name="grad_pre",
    )(g, hbm(down), hbm(pre), hbm(dg), u)


def sums_row(a, b):
    rows = []
    for t in (a, b):
        s = jnp.broadcast_to(jnp.sum(t, axis=1, keepdims=True), (NP, 128))
        rows.append(jnp.transpose(s)[0:1, :])
    return jnp.concatenate(rows, axis=1)


def keep_kernel(src, dst, sem):
    copy = pltpu.make_async_copy(src, dst, sem)
    copy.start()
    copy.wait()


def keep(a):
    return pl.pallas_call(
        keep_kernel,
        out_shape=pltpu.VMEM(a.shape, a.dtype),
        in_specs=[pl.BlockSpec(memory_space=pltpu.HBM)],
        out_specs=pl.BlockSpec(memory_space=pltpu.VMEM),
        scratch_shapes=[pltpu.SemaphoreType.DMA],
        compiler_params=params(12),
        cost_estimate=pl.CostEstimate(flops=0, bytes_accessed=2 * a.size * 2, transcendentals=0),
        name="keep",
    )(a)


def nt_kernel(steps, other, kept, with_sums, first_add, stacked, info, lhs_ref, rhs_ref, *refs):
    refs = list(refs)
    s_ref = refs.pop(0) if with_sums else None
    add_ref = refs.pop(0) if first_add is not None else None
    core = 1 - info[3] if other else info[3]
    n = len(steps)
    rows = [pl.ds(pl.multiple_of((2 * ((info[2] + k) % NX) + core) * W, W), W) for k in steps]
    if not kept:
        buf, sem = refs[-2:]
        copies = [pltpu.make_async_copy(rhs_ref.at[rows[i], :], buf.at[i], sem.at[i]) for i in range(n)]
        for cp in copies:
            cp.start()
    for i in range(n):
        if not kept:
            copies[i].wait()
        out = refs[0].at[i] if stacked else refs[i]
        acc = dot(lhs_ref[...], rhs_ref[rows[i], :] if kept else buf[i], NT)
        if first_add is not None:
            acc = acc + add_ref[first_add + i, :NP, :].astype(F32)
        out[:NP, :] = acc.astype(BF)
        if with_sums:
            if first_add is not None:
                out[NP:, :] = ride(unride(s_ref[...]) + unride(add_ref[first_add + i, NP:, :]))
            else:
                out[NP:, :] = s_ref[...]


def nt_call(steps, other, kept, info, lhs, rhs, sums=None, add=None, first_add=None, stacked=False, name=None):
    n = len(steps)
    rows = EXT if sums is not None else NP
    args = [info, lhs, rhs if kept else hbm(rhs)]
    in_specs = [SM, VM, VM if kept else pl.BlockSpec(memory_space=pltpu.HBM)]
    for extra in (sums, add):
        if extra is not None:
            args.append(extra)
            in_specs.append(VM)
    return pl.pallas_call(
        functools.partial(nt_kernel, steps, other, kept, sums is not None, first_add, stacked),
        in_specs=in_specs,
        out_specs=VM if stacked else tuple([VM] * n),
        out_shape=sds((n, rows, W), BF) if stacked else tuple([sds((rows, W), BF)] * n),
        scratch_shapes=[] if kept else [pltpu.VMEM((n, W, HID), BF), pltpu.SemaphoreType.DMA((n,))],
        compiler_params=params(BIG),
        cost_estimate=pl.CostEstimate(flops=2 * NP * HID * W * n, bytes_accessed=n << 20, transcendentals=0),
        name=name,
    )(*args)


def tensor_scatter(info, lhs, rhs, sums, name, kept):
    o = send(nt_call((2, 1, 3, 0), True, kept, info, lhs, rhs, sums, stacked=True, name=name + "_o"), "c", 1)
    far, = nt_call((2,), False, kept, info, lhs, rhs, sums, o, 0, name=name + "_f")
    lhs, far = lax.optimization_barrier((lhs, far))
    far = send(far, "x", 2)
    ahead, behind, own = nt_call((1, 3, 0), False, kept, info, lhs, rhs, sums, o, 1, name=name + "_n")
    return own, send(ahead, "x", 1), send(behind, "x", -1), far


def bwd_kernel(own_ref, p1_ref, p2_ref, p3_ref, agg_ref, st_ref, gain_ref, g_ref, emb_ref, attn_ref, x_ref, q_ref,
               *rest):
    out_ref, acc = rest
    parts = (own_ref, p1_ref, p2_ref, p3_ref)
    expand = head_mask(BF)
    scale = HEAD ** -0.5
    qrow = q_ref[...].astype(F32) * scale
    gain = gain_ref[...].astype(F32)
    sums = sum(unride(p[NP:, :]) for p in parts)
    cols = []
    for k in range(2):
        row = sums[:, k * NP:(k + 1) * NP] * (1.0 / D)
        cols.append(jnp.transpose(jnp.broadcast_to(row, (128, NP))))
    expand2 = jnp.concatenate([expand, expand], axis=0)
    rows = 128
    group = lane_group((rows, 128))
    group2 = lax.broadcasted_iota(jnp.int32, (rows, 256), 1) % 128 // 16
    gq = jnp.zeros((8, W), F32)
    for r in range(NP // rows):
        at = slice(r * rows, (r + 1) * rows)
        mean, inv = st_ref[0, at, 0:1], st_ref[1, at, 0:1]
        xh = (agg_ref[at, :].astype(F32) - mean) * inv
        gs = sum(p[at, :].astype(F32) for p in parts) * gain
        ga = g_ref[at, :].astype(F32) + inv * (gs - cols[0][at, 0:1] - xh * cols[1][at, 0:1])
        gab = ga.astype(BF).astype(F32)
        gattn = jnp.zeros((rows, 128), F32)
        for j in range(VMAX):
            prod = gab * emb_ref[j, at, :].astype(F32)
            hi = prod.astype(BF)
            low = (prod - hi.astype(F32)).astype(BF)
            both = dot(hi, expand, NT) + dot(low, expand, NT)
            gattn = jnp.where(group == j, both, gattn)
        attn = attn_ref[at, :]
        gscore = attn * (gattn - over_slots(jnp.add, attn * gattn))
        ahi = attn.astype(BF)
        alow = (attn - ahi.astype(F32)).astype(BF)
        shi = gscore.astype(BF)
        slow = (gscore - shi.astype(F32)).astype(BF)
        a2 = jnp.concatenate([ahi, alow], axis=1)
        s2 = jnp.concatenate([shi, slow], axis=1)
        zero = jnp.zeros_like(a2)
        xt = jnp.transpose(x_ref[at, :].astype(F32)).astype(BF)
        pick_row = lax.broadcasted_iota(jnp.int32, (256, 128), 0)
        pick_col = lax.broadcasted_iota(jnp.int32, (256, 128), 1)
        pixel = 16 * (pick_row // 32) + 2 * (pick_row % 32 // 4) + pick_row % 4
        chosen = jnp.where((pick_col == pixel) & (pick_row % 4 < 2), 1.0, 0.0).astype(BF)
        lhs_all = jnp.where(pick_row % 4 < 2, dot(chosen, xt), 1.0).astype(BF)
        for j in range(VMAX):
            pick = group2 == j
            a_w = dot(jnp.where(pick, a2, zero), expand2)
            s_w = dot(jnp.where(pick, s2, zero), expand2)
            ge = (a_w * ga + s_w * qrow).astype(BF)
            e = emb_ref[j, at, :].astype(F32)
            part_q = s_w.astype(BF).astype(F32) * e
            for k in range(rows // 8):
                gq = gq + part_q[8 * k:8 * k + 8, :]
            got = dot(lhs_all[32 * j:32 * j + 32, :], ge)
            for z in range(NZ):
                to = slice(32 * z + 4 * j, 32 * z + 4 * j + 4)
                if r == 0:
                    acc[to, :] = got[4 * z:4 * z + 4]
                else:
                    acc[to, :] += got[4 * z:4 * z + 4]
    gq = jnp.sum(gq, axis=0, keepdims=True) * scale
    for z in range(NZ):
        acc[32 * z + 3:32 * z + 4, :] = gq
        for y in range(NY):
            out_ref[NZ * y + z] = acc[32 * z:32 * z + 32, 128 * y:128 * y + 128].astype(BF)


def attention_backward(gn, agg, st, gain, g, emb, attn, x, q):
    return call(
        bwd_kernel, sds((NY * NZ, 32, 128), BF), 0, 12, [pltpu.VMEM((256, W), F32)], mib=BIG,
        flops=2 * 6 * 8 * 256 * 128 * 512, nbytes=5 << 20, name="attn_bwd",
    )(gn[0], *map(hbm, gn[1:]), agg, st, gain, hbm(g), emb, attn, x, q)


def sum_kernel(destination, counts, ids, got_ref, main_ref, rest_ref, acc, bias, pair, query, inverse):
    acc[...] = jnp.zeros_like(acc)
    for i in range(NY * NZ):
        inverse[destination[i]] = i
    total = jnp.zeros((8, 128), F32)
    for rank in range(NY * NZ):
        sample = inverse[rank]
        live = counts[sample]
        data = got_ref[rank].astype(F32)
        total = total + data[0:8]
        for j in range(VMAX):
            v = ids[sample * VMAX + j]

            @pl.when(j < live)
            def _():
                acc[v, 0:4, :] += data[4 * j:4 * j + 4]
    query[...] = total
    for v in range(NVAR):
        pair[2 * v:2 * v + 2, :] = acc[v, 0:2, :]
        bias[v:v + 1, :] = acc[v, 2:3, :]
    for z in range(NZ):
        main_ref[z] = pair[...].astype(BF)
    rest_ref[0:48, :] = bias[...].astype(BF)
    rest_ref[48:64, :] = jnp.broadcast_to(query[3:4, :], (16, 128)).astype(BF)


def spread_kernel(info, *refs):
    pieces = refs[0:4]
    ge_ref, gv_ref, gq_ref, pair = refs[4:]
    for k, piece in enumerate(pieces):
        col = pl.ds(pl.multiple_of((info[0] + (0, 3, 1, 2)[k]) % NY * 128, 128), 128)
        for z in range(NZ):
            pair[...] = piece[96 * z:96 * z + 96, :].astype(F32)
            for v in range(NVAR):
                ge_ref[v, 2 * z:2 * z + 2, col] = pair[2 * v:2 * v + 2, :]
        gv_ref[:, col] = piece[768:816, :].astype(F32)
        gq_ref[:, col] = piece[816:832, :].astype(F32)[0:1]


def gradient_exchange(info, routing, outs):
    got = lax.all_to_all(outs, ("y", "z"), 0, 0, tiled=True)
    main, rest = call(
        sum_kernel, (sds((NZ, 96, 128), BF), sds((64, 128), BF)), 3, 1,
        [pltpu.VMEM((NVAR, 8, 128), F32), pltpu.VMEM((NVAR, 128), F32), pltpu.VMEM((96, 128), F32),
         pltpu.VMEM((8, 128), F32), pltpu.SMEM((NY * NZ,), jnp.int32)],
        mib=BIG, flops=1 << 20, nbytes=2 << 20, name="slot_sum",
    )(*routing, got)
    main = lax.all_to_all(main, "z", 0, 0, tiled=True)
    both = jnp.concatenate([main.reshape(NZ * 96, 128), rest], axis=0)
    pieces = [both, send(both, "y", 1), send(both, "y", -1), send(both, "y", 2)]
    return call(
        spread_kernel, (sds((NVAR, PP, W), F32), sds((NVAR, W), F32), sds((1, W), F32)), 1, 4,
        [pltpu.VMEM((96, 128), F32)], mib=BIG, flops=1 << 20, nbytes=3 << 20, name="spread",
    )(info, both, *map(hbm, pieces[1:]))


def mix_kernel(agg_ref, own, p1, p2, p3, out_ref):
    total = agg_ref[:NP, :].astype(F32)
    for p in (own, p1, p2, p3):
        total = total + p[...].astype(F32)
    out_ref[0] = total.astype(BF)


def pixel_gather(own):
    mine = jnp.stack([own, send(own, "x", 1), send(own, "x", -1), send(own, "x", 2)])
    return mine, send(mine, "c", 1)


def local(pixels, counts, var_ids, destination, embed_weight, var_embed, agg_query, ln_gain, fc_up, fc_down, cotangent):
    y, z, x, c = (lax.axis_index(a) for a in ("y", "z", "x", "c"))
    info = jnp.stack([y, z, x, c]).astype(jnp.int32)
    routing = destination, counts, var_ids.reshape(-1)
    g_own = cotangent[0]
    down = lax.all_gather(fc_down, ("y", "z"), axis=0, tiled=True)

    to_rank = destination[None, :] == jnp.arange(NY * NZ)[:, None]
    ordered = dot(to_rank.astype(BF), pixels[:, 0, :]).astype(BF)
    mine = lax.all_to_all(ordered, ("y", "z"), 0, 0, tiled=True)
    q, info, mine = lax.optimization_barrier((agg_query.reshape(1, W), info, mine))
    mine, swapped = pixel_gather(mine)

    agg, emb, attn, patches = attention_forward(info, routing, (mine, swapped), embed_weight, var_embed, q, ln_gain)
    pieces = tensor_gather(agg)
    pre, dg, hid, u, st = up_call(info, pieces, fc_up)
    g_late, _ = lax.optimization_barrier((g_own, u))
    g_pieces = tensor_gather(g_late)
    up_src, _ = lax.optimization_barrier((fc_up, g_pieces[4]))
    up_kept = keep(up_src)
    down, up_kept, g_whole = lax.optimization_barrier((down, up_kept, join(info, g_pieces)))
    gp, sums = grad_pre(g_whole, down, pre, dg, u)
    gn = tensor_scatter(info, gp, up_kept, sums, "gn", True)
    mark, _ = lax.optimization_barrier((sums, gn[0]))
    hid, _ = lax.optimization_barrier((hid, send(mark, "c", 1)))
    br = tensor_scatter(info, hid, down, None, "br", False)
    gn, br = list(gn), list(br)
    gn[0], br[0] = lax.optimization_barrier((gn[0], br[0]))
    outs = attention_backward(gn, agg, st, ln_gain, g_own, emb, attn, patches, q)
    mixed = call(mix_kernel, sds((1, NP, W), BF), 0, 5, mib=BIG, nbytes=1 << 20, name="mix")(
        agg, br[0], *map(hbm, br[1:]))
    ge, gv, gq = gradient_exchange(info, routing, outs)
    return mixed, ge, gv, gq.reshape(W)


def solution(mesh):
    fine = Mesh(mesh.devices.reshape(NY, NZ, NX, NC), ("y", "z", "x", "c"))
    dp, tensor = ("y", "z"), ("x", "c")
    in_specs = (
        P(None, dp + tensor, None), P(), P(), P(), P(None, None, tensor), P(None, tensor), P(tensor),
        P(None, tensor), P(None, tensor), P(dp, tensor), P(dp, None, tensor),
    )
    out_specs = (P(dp, None, tensor), P(None, None, tensor), P(None, tensor), P(tensor))
    return jax.shard_map(local, mesh=fine, in_specs=in_specs, out_specs=out_specs, check_vma=False)
```

```python
import functools

import jax
import jax.numpy as jnp
from jax import lax
from jax.experimental import pallas as pl
from jax.experimental.pallas import tpu as pltpu
from jax.sharding import Mesh, PartitionSpec as P

HEAD = 128
VMAX = 8
PP = 16
NVAR = 48
D = 4096
FF = 8192
NP = 256
W = 512
HID = 1024
EXT = NP + 16
BF = jnp.bfloat16
F32 = jnp.float32
NT = (((1,), (1,)), ((), ()))
VM = pl.BlockSpec(memory_space=pltpu.VMEM)
SM = pl.BlockSpec(memory_space=pltpu.SMEM)
NX, NY, NZ, NC = 4, 4, 8, 2
BIG = 16


def params(mib):
    return pltpu.CompilerParams(vmem_limit_bytes=mib << 20)


def call(kernel, outs, n_smem, n_vmem, scratch=(), mib=BIG, flops=0, nbytes=0, name=None):
    single = not isinstance(outs, (list, tuple))
    return pl.pallas_call(
        kernel,
        out_shape=outs if single else tuple(outs),
        in_specs=[SM] * n_smem + [VM] * n_vmem,
        out_specs=VM if single else tuple([VM] * len(outs)),
        scratch_shapes=list(scratch),
        compiler_params=params(mib),
        cost_estimate=pl.CostEstimate(flops=flops, bytes_accessed=nbytes, transcendentals=0),
        name=name,
    )


def sds(shape, dtype):
    return jax.ShapeDtypeStruct(shape, dtype)


def hbm(a):
    return pltpu.with_memory_space_constraint(a, pltpu.HBM)


def send(a, axis, k):
    n = {"x": NX, "y": NY, "z": NZ, "c": NC}[axis]
    return lax.ppermute(a, axis, [(i, (i + k) % n) for i in range(n)])


def around(a, axis):
    n = {"x": NX, "y": NY, "z": NZ}[axis]
    steps = [(2 * i + k, 2 * ((i + 1 - 2 * k) % n) + k) for i in range(n) for k in range(NC)]
    return lax.ppermute(a, (axis, "c"), steps)


def dot(a, b, dims=(((1,), (0,)), ((), ()))):
    return lax.dot_general(a, b, dims, preferred_element_type=F32)


def lane_group(shape):
    return lax.broadcasted_iota(jnp.int32, shape, 1) // 16


def head_mask(dtype):
    row = lax.broadcasted_iota(jnp.int32, (128, W), 0)
    col = lax.broadcasted_iota(jnp.int32, (128, W), 1)
    return jnp.where(row % 16 == col // HEAD, 1.0, 0.0).astype(dtype)


def over_slots(op, a):
    for shift in (16, 32, 64):
        a = op(a, pltpu.roll(a, shift, 1))
    return a


def find(destination, rank):
    return lax.fori_loop(0, NY * NZ, lambda i, s: jnp.where(destination[i] == rank, i, s), 0)


def fwd_kernel(info, destination, counts, var_ids, xa_ref, xb_ref, ew_ref, ve_ref, q_ref, gain_ref,
               agg_ref, emb_ref, attn_ref, x_ref, wblk, wsem):
    copies = []
    sample = find(destination, info[0] * NZ + info[1])
    count = counts[sample]
    ids = [var_ids[sample * VMAX + j] for j in range(VMAX)]
    for j in range(VMAX):
        copies.append(pltpu.make_async_copy(ew_ref.at[ids[j]], wblk.at[j, pl.ds(16 * j, 16), :], wsem.at[j]))
    zero = jnp.zeros((16, W), BF)
    for j in range(VMAX):
        for k in range(VMAX):
            if k != j:
                wblk[j, 16 * k:16 * (k + 1), :] = zero
    for cp in copies:
        cp.start()
    col = lax.broadcasted_iota(jnp.int32, (1, NP), 1)
    device = jnp.zeros((1, NP), jnp.int32)
    for k in range(8):
        chip, core = (info[2] + (0, 3, 1, 2)[k % 4]) % 4, (info[3] + k // 4) % 2
        device = jnp.where(col // 32 == k, 2 * chip + core, device)
    row = lax.broadcasted_iota(jnp.int32, (NP, NP), 0)
    order = jnp.where(row == 8 * (col % 32) + device, 1.0, 0.0).astype(BF)
    pieces = jnp.concatenate([r[k] for r in (xa_ref, xb_ref) for k in range(4)], axis=0)
    x_ref[...] = dot(order, pieces).astype(BF)
    at_slot = lax.broadcasted_iota(jnp.int32, (16, NVAR), 0)
    at_var = lax.broadcasted_iota(jnp.int32, (16, NVAR), 1)
    onehot = jnp.zeros((16, NVAR), F32)
    for j in range(VMAX):
        onehot = jnp.where((at_slot == j) & (at_var == ids[j]), 1.0, onehot)
    bias = dot(onehot.astype(BF), ve_ref[...])
    expand = head_mask(BF)
    qmat = (expand.astype(F32) * q_ref[...].astype(F32)).astype(BF)
    for cp in copies:
        cp.wait()
    rows = 128
    group = lane_group((rows, 128))
    for r in range(NP // rows):
        at = slice(r * rows, (r + 1) * rows)
        x = x_ref[at, :]
        scores = jnp.zeros((rows, 128), F32)
        for j in range(VMAX):
            e = (dot(x, wblk[j]) + bias[j:j + 1, :]).astype(BF)
            emb_ref[j, at, :] = e
            scores = jnp.where(group == j, dot(e, qmat, NT), scores)
        scores = scores * (HEAD ** -0.5)
        scores = jnp.where(group < count, scores, -jnp.inf)
        top = over_slots(jnp.maximum, scores)
        raised = jnp.exp(scores - top)
        attn = raised / over_slots(jnp.add, raised)
        attn_ref[at, :] = attn
        attn_b = attn.astype(BF)
        total = jnp.zeros((rows, W), F32)
        for j in range(VMAX):
            wide = dot(jnp.where(group == j, attn_b, jnp.zeros_like(attn_b)), expand)
            total = total + wide * emb_ref[j, at, :].astype(F32)
        agg_ref[at, :] = total.astype(BF)
    agg_ref[NP:EXT, :] = jnp.broadcast_to(gain_ref[...], (16, W))


def attention_forward(info, routing, xs, ew, ve, q, gain):
    return pl.pallas_call(
        fwd_kernel,
        out_shape=(sds((EXT, W), BF), sds((VMAX, NP, W), BF), sds((NP, 128), F32), sds((NP, 128), BF)),
        in_specs=[SM] * 4 + [VM, VM, pl.BlockSpec(memory_space=pl.ANY), VM, VM, VM],
        out_specs=(VM, VM, VM, VM),
        scratch_shapes=[pltpu.VMEM((VMAX, 128, W), BF), pltpu.SemaphoreType.DMA((VMAX,))],
        compiler_params=params(BIG),
        cost_estimate=pl.CostEstimate(flops=2 * 3 * 8 * 256 * 128 * 512, bytes_accessed=4 << 20, transcendentals=0),
        name="attn_fwd",
    )(info, *routing, *xs, ew, ve, q, gain)


def tensor_gather(a):
    first = around(a, "x")
    other = send(a, "c", 1)
    second = around(other, "x")
    far = around(first, "x")
    return a, other, first, second, far, send(first, "c", 1), send(second, "c", 1), send(far, "c", 1)


def blocks_of(info, refs):
    x, c = info[2], info[3]
    d = 1 - 2 * c
    back, fore, opposite = (x + 4 - d) % 4, (x + 4 + d) % 4, (x + 2) % 4
    place = ((x, c), (x, 1 - c), (back, c), (back, 1 - c), (opposite, c), (fore, 1 - c), (fore, c), (opposite, 1 - c))
    return [(chip, core, ref) for (chip, core), ref in zip(place, refs)]


def up_kernel(info, *refs):
    pieces, up_ref = refs[:8], refs[8]
    pre_ref, dg_ref, hid_ref, u_ref, st_ref, nrm = refs[9:]

    @pl.when(pl.program_id(0) == 0)
    def _():
        blocks = [(2 * chip + core, p) for chip, core, p in blocks_of(info, pieces)]
        for r in range(4):
            lo, hi = 64 * r, 64 * r + 64
            total = jnp.zeros((64, W), F32)
            for _, p in blocks:
                total = total + p[lo:hi, :].astype(F32)
            mean = jnp.sum(total, axis=1, keepdims=True) * (1.0 / D)
            total = jnp.zeros((64, W), F32)
            for _, p in blocks:
                d = p[lo:hi, :].astype(F32) - mean
                total = total + d * d
            inv = lax.rsqrt(jnp.sum(total, axis=1, keepdims=True) * (1.0 / D) + 1e-05)
            st_ref[0, lo:hi, :] = jnp.broadcast_to(mean, (64, 128))
            st_ref[1, lo:hi, :] = jnp.broadcast_to(inv, (64, 128))
            for b, p in blocks:
                gain = p[NP:EXT, :][0:1, :].astype(F32)
                col = pl.ds(pl.multiple_of(b * W, W), W)
                nrm[lo:hi, col] = ((p[lo:hi, :].astype(F32) - mean) * inv * gain).astype(BF)
        for b, p in blocks:
            nrm[NP:EXT, pl.ds(pl.multiple_of(b * W, W), W)] = p[NP:EXT, :]

    acc = dot(nrm[...], up_ref[...])
    x = acc[:NP]
    c = 0.7978845608028654
    th = jnp.tanh(c * (x + 0.044715 * (x * x * x)))
    pre_ref[...] = x
    hid_ref[...] = (0.5 * x * (1.0 + th)).astype(BF)
    dg_ref[...] = 0.5 * (1.0 + th) + 0.5 * x * (1.0 - th * th) * (c * (1.0 + 3 * 0.044715 * (x * x)))
    u_ref[...] = acc[NP:NP + 8]


def up_call(info, pieces, fc_up):
    n = 4
    w = HID // n
    whole = [pl.BlockSpec(p.shape, lambda i: (0, 0)) for p in pieces]
    return pl.pallas_call(
        up_kernel,
        grid=(n,),
        out_shape=(sds((NP, HID), F32), sds((NP, HID), F32), sds((NP, HID), BF), sds((8, HID), F32), sds((2, NP, 128), F32)),
        in_specs=[SM] + whole + [pl.BlockSpec((D, w), lambda i: (0, i))],
        out_specs=(
            pl.BlockSpec((NP, w), lambda i: (0, i)), pl.BlockSpec((NP, w), lambda i: (0, i)),
            pl.BlockSpec((NP, w), lambda i: (0, i)), pl.BlockSpec((8, w), lambda i: (0, i)),
            pl.BlockSpec((2, NP, 128), lambda i: (0, 0, 0)),
        ),
        scratch_shapes=[pltpu.VMEM((EXT, D), BF)],
        compiler_params=params(BIG),
        cost_estimate=pl.CostEstimate(flops=2 * EXT * D * HID, bytes_accessed=16 << 20, transcendentals=0),
        name="ln_up",
    )(info, *map(hbm, pieces), hbm(fc_up))


def split3(row):
    hi = row.astype(BF).astype(F32)
    mid = (row - hi).astype(BF).astype(F32)
    return hi, mid, row - hi - mid


def ride(row):
    hi, mid, low = split3(row)
    at = lax.broadcasted_iota(jnp.int32, (16, W), 0)
    tile = jnp.where(at == 0, hi, jnp.where(at == 1, mid, jnp.where(at == 2, low, 0.0)))
    return tile.astype(BF)


def unride(tile):
    return jnp.sum(tile.astype(F32), axis=0, keepdims=True)


def join_kernel(info, *refs):
    pieces, out = refs[:8], refs[8]
    for chip, core, p in blocks_of(info, pieces):
        out[:, pl.ds(pl.multiple_of((2 * chip + core) * W, W), W)] = p[...]


def join(info, pieces):
    return call(join_kernel, sds((NP, D), BF), 1, 8, mib=BIG, nbytes=4 << 20, name="join")(info, *map(hbm, pieces))


def gh_kernel(g, down_ref, pre_ref, dg_ref, u_ref, gp_ref, s_ref, tot):
    i = pl.program_id(0)

    @pl.when(i == 0)
    def _():
        tot[...] = jnp.zeros_like(tot)

    gh = dot(g[...], down_ref[...])
    gp = (gh * dg_ref[...]).astype(BF)
    gp_ref[...] = gp
    gpf = gp.astype(F32)
    a = gpf * u_ref[0:1, :]
    b = gpf * pre_ref[...]
    tot[0] += a[:, :128] + a[:, 128:]
    tot[1] += b[:, :128] + b[:, 128:]

    @pl.when(i == pl.num_programs(0) - 1)
    def _():
        s_ref[...] = ride(sums_row(tot[0], tot[1]))


def grad_pre(g, down, pre, dg, u):
    n = 4
    w = HID // n

    def col(r):
        return pl.BlockSpec((r, w), lambda i: (0, i))

    return pl.pallas_call(
        gh_kernel,
        grid=(n,),
        out_shape=(sds((NP, HID), BF), sds((16, W), BF)),
        in_specs=[VM, col(D), col(NP), col(NP), col(8)],
        out_specs=(col(NP), pl.BlockSpec((16, W), lambda i: (0, 0))),
        scratch_shapes=[pltpu.VMEM((2, NP, 128), F32)],
        compiler_params=params(BIG),
        cost_estimate=pl.CostEstimate(flops=2 * NP * D * HID, bytes_accessed=12 << 20, transcendentals=0),
        name="grad_pre",
    )(g, hbm(down), hbm(pre), hbm(dg), u)


def sums_row(a, b):
    rows = []
    for t in (a, b):
        s = jnp.broadcast_to(jnp.sum(t, axis=1, keepdims=True), (NP, 128))
        rows.append(jnp.transpose(s)[0:1, :])
    return jnp.concatenate(rows, axis=1)


def keep_kernel(src, dst, sem):
    copy = pltpu.make_async_copy(src, dst, sem)
    copy.start()
    copy.wait()


def keep(a):
    return pl.pallas_call(
        keep_kernel,
        out_shape=pltpu.VMEM(a.shape, a.dtype),
        in_specs=[pl.BlockSpec(memory_space=pltpu.HBM)],
        out_specs=pl.BlockSpec(memory_space=pltpu.VMEM),
        scratch_shapes=[pltpu.SemaphoreType.DMA],
        compiler_params=params(12),
        cost_estimate=pl.CostEstimate(flops=0, bytes_accessed=2 * a.size * 2, transcendentals=0),
        name="keep",
    )(a)


def nt_kernel(steps, other, kept, with_sums, first_add, stacked, info, lhs_ref, rhs_ref, *refs):
    refs = list(refs)
    s_ref = refs.pop(0) if with_sums else None
    add_ref = refs.pop(0) if first_add is not None else None
    core = 1 - info[3] if other else info[3]
    n = len(steps)
    rows = [pl.ds(pl.multiple_of((2 * ((info[2] + k) % NX) + core) * W, W), W) for k in steps]
    if not kept:
        buf, sem = refs[-2:]
        copies = [pltpu.make_async_copy(rhs_ref.at[rows[i], :], buf.at[i], sem.at[i]) for i in range(n)]
        for cp in copies:
            cp.start()
    for i in range(n):
        if not kept:
            copies[i].wait()
        out = refs[0].at[i] if stacked else refs[i]
        acc = dot(lhs_ref[...], rhs_ref[rows[i], :] if kept else buf[i], NT)
        if first_add is not None:
            acc = acc + add_ref[first_add + i, :NP, :].astype(F32)
        out[:NP, :] = acc.astype(BF)
        if with_sums:
            if first_add is not None:
                out[NP:, :] = ride(unride(s_ref[...]) + unride(add_ref[first_add + i, NP:, :]))
            else:
                out[NP:, :] = s_ref[...]


def nt_call(steps, other, kept, info, lhs, rhs, sums=None, add=None, first_add=None, stacked=False, name=None):
    n = len(steps)
    rows = EXT if sums is not None else NP
    args = [info, lhs, rhs if kept else hbm(rhs)]
    in_specs = [SM, VM, VM if kept else pl.BlockSpec(memory_space=pltpu.HBM)]
    for extra in (sums, add):
        if extra is not None:
            args.append(extra)
            in_specs.append(VM)
    return pl.pallas_call(
        functools.partial(nt_kernel, steps, other, kept, sums is not None, first_add, stacked),
        in_specs=in_specs,
        out_specs=VM if stacked else tuple([VM] * n),
        out_shape=sds((n, rows, W), BF) if stacked else tuple([sds((rows, W), BF)] * n),
        scratch_shapes=[] if kept else [pltpu.VMEM((n, W, HID), BF), pltpu.SemaphoreType.DMA((n,))],
        compiler_params=params(BIG),
        cost_estimate=pl.CostEstimate(flops=2 * NP * HID * W * n, bytes_accessed=n << 20, transcendentals=0),
        name=name,
    )(*args)


def half_kernel(a_ref, b_ref, out_ref):
    out_ref[:NP, :] = a_ref[:NP, :].astype(F32) + b_ref[:NP, :].astype(F32)
    if a_ref.shape[0] > NP:
        at = lax.broadcasted_iota(jnp.int32, (16, W), 0)
        out_ref[NP:, :] = jnp.where(at == 0, unride(a_ref[NP:, :]) + unride(b_ref[NP:, :]), 0.0)


def tensor_scatter(info, lhs, rhs, sums, name, kept):
    o = send(nt_call((2, 1, 3, 0), True, kept, info, lhs, rhs, sums, stacked=True, name=name + "_o"), "c", 1)
    far, = nt_call((2,), False, kept, info, lhs, rhs, sums, o, 0, name=name + "_f")
    lhs, far = lax.optimization_barrier((lhs, far))
    far = send(far, "x", 2)
    ahead, behind, own = nt_call((1, 3, 0), False, kept, info, lhs, rhs, sums, o, 1, name=name + "_n")
    return call(half_kernel, sds(own.shape, F32), 0, 2, mib=BIG, nbytes=1 << 20, name=name + "_p")(own, far), send(
        ahead, "x", 1), send(behind, "x", -1)


def rows_kernel(x_ref, out_ref):
    row = lax.broadcasted_iota(jnp.int32, (256, 128), 0)
    col = lax.broadcasted_iota(jnp.int32, (256, 128), 1)
    pixel = 16 * (row // 32) + 2 * (row % 32 // 4) + row % 4
    chosen = jnp.where((col == pixel) & (row % 4 < 2), 1.0, 0.0).astype(BF)
    got = dot(chosen, x_ref[...], NT)
    at = lax.broadcasted_iota(jnp.int32, (256, NP), 0)
    out_ref[...] = jnp.where(at % 4 < 2, got, 1.0).astype(BF)


def bwd_kernel(own_ref, p1_ref, p2_ref, agg_ref, st_ref, gain_ref, g_ref, emb_ref, attn_ref, x_ref, q_ref,
               *rest):
    out_ref, acc, gq = rest
    parts = (own_ref, p1_ref, p2_ref)
    expand = head_mask(BF)
    scale = HEAD ** -0.5
    qrow = q_ref[...].astype(F32) * scale
    gain = gain_ref[...].astype(F32)
    sums = sum(unride(p[NP:, :]) for p in parts)
    cols = []
    for k in range(2):
        row = sums[:, k * NP:(k + 1) * NP] * (1.0 / D)
        cols.append(jnp.transpose(jnp.broadcast_to(row, (128, NP))))
    expand2 = jnp.concatenate([expand, expand], axis=0)
    rows = NP
    group = lane_group((rows, 128))
    group2 = lax.broadcasted_iota(jnp.int32, (rows, 256), 1) % 128 // 16
    for r in range(NP // rows):
        at = slice(r * rows, (r + 1) * rows)
        mean, inv = st_ref[0, at, 0:1], st_ref[1, at, 0:1]
        xh = (agg_ref[at, :].astype(F32) - mean) * inv
        gs = sum(p[at, :].astype(F32) for p in parts) * gain
        ga = g_ref[at, :].astype(F32) + inv * (gs - cols[0][at, 0:1] - xh * cols[1][at, 0:1])
        gab = ga.astype(BF).astype(F32)
        gattn = jnp.zeros((rows, 128), F32)
        for j in range(VMAX):
            prod = gab * emb_ref[j, at, :].astype(F32)
            hi = prod.astype(BF)
            low = (prod - hi.astype(F32)).astype(BF)
            both = dot(hi, expand, NT) + dot(low, expand, NT)
            gattn = jnp.where(group == j, both, gattn)
        attn = attn_ref[at, :]
        gscore = attn * (gattn - over_slots(jnp.add, attn * gattn))
        ahi = attn.astype(BF)
        alow = (attn - ahi.astype(F32)).astype(BF)
        shi = gscore.astype(BF)
        slow = (gscore - shi.astype(F32)).astype(BF)
        a2 = jnp.concatenate([ahi, alow], axis=1)
        s2 = jnp.concatenate([shi, slow], axis=1)
        zero = jnp.zeros_like(a2)
        gst = jnp.transpose(shi.astype(F32)).astype(BF)
        for j in range(VMAX):
            pick = group2 == j
            a_w = dot(jnp.where(pick, a2, zero), expand2)
            s_w = dot(jnp.where(pick, s2, zero), expand2)
            ge = (a_w * ga + s_w * qrow).astype(BF)
            mine = slice(16 * j, 16 * j + 16)
            part_q = dot(gst[mine, :], emb_ref[j, at, :])
            gq[mine, :] = part_q if r == 0 else gq[mine, :] + part_q
            got = dot(x_ref[32 * j:32 * j + 32, at], ge)
            for z in range(NZ):
                to = slice(32 * z + 4 * j, 32 * z + 4 * j + 4)
                if r == 0:
                    acc[to, :] = got[4 * z:4 * z + 4]
                else:
                    acc[to, :] += got[4 * z:4 * z + 4]
    total_q = jnp.sum(gq[...] * expand.astype(F32), axis=0, keepdims=True) * scale
    for z in range(NZ):
        acc[32 * z + 3:32 * z + 4, :] = total_q
        for y in range(NY):
            out_ref[NZ * y + z] = acc[32 * z:32 * z + 32, 128 * y:128 * y + 128].astype(BF)


def attention_backward(gn, agg, st, gain, g, emb, attn, x, q):
    return call(
        bwd_kernel, sds((NY * NZ, 32, 128), BF), 0, 11, [pltpu.VMEM((256, W), F32), pltpu.VMEM((128, W), F32)], mib=BIG,
        flops=2 * 6 * 8 * 256 * 128 * 512, nbytes=5 << 20, name="attn_bwd",
    )(gn[0], *map(hbm, gn[1:]), agg, st, gain, hbm(g), emb, attn, x, q)


def sum_kernel(destination, counts, ids, got_ref, main_ref, rest_ref, acc, bias, pair, query, inverse):
    acc[...] = jnp.zeros_like(acc)
    for i in range(NY * NZ):
        inverse[destination[i]] = i
    total = jnp.zeros((8, 128), F32)
    for rank in range(NY * NZ):
        sample = inverse[rank]
        live = counts[sample]
        data = got_ref[rank].astype(F32)
        total = total + data[0:8]
        for j in range(VMAX):
            v = jnp.where(j < live, ids[sample * VMAX + j], NVAR)
            acc[v, 0:4, :] += data[4 * j:4 * j + 4]
    query[...] = total
    for v in range(NVAR):
        pair[2 * v:2 * v + 2, :] = acc[v, 0:2, :]
        bias[v:v + 1, :] = acc[v, 2:3, :]
    for z in range(NZ):
        main_ref[z] = pair[...].astype(BF)
    rest_ref[0:48, :] = bias[...].astype(BF)
    rest_ref[48:64, :] = jnp.broadcast_to(query[3:4, :], (16, 128)).astype(BF)


def spread_kernel(info, *refs):
    pieces = refs[0:4]
    ge_ref, gv_ref, gq_ref, pair = refs[4:]
    for k, piece in enumerate(pieces):
        col = pl.ds(pl.multiple_of((info[0] + (0, 3, 1, 2)[k]) % NY * 128, 128), 128)
        for z in range(NZ):
            pair[...] = piece[96 * z:96 * z + 96, :].astype(F32)
            for v in range(NVAR):
                ge_ref[v, 2 * z:2 * z + 2, col] = pair[2 * v:2 * v + 2, :]
        gv_ref[:, col] = piece[768:816, :].astype(F32)
        gq_ref[:, col] = piece[816:832, :].astype(F32)[0:1]


def gradient_exchange(info, routing, outs):
    got = lax.all_to_all(outs, ("y", "z"), 0, 0, tiled=True)
    main, rest = call(
        sum_kernel, (sds((NZ, 96, 128), BF), sds((64, 128), BF)), 3, 1,
        [pltpu.VMEM((NVAR + 1, 8, 128), F32), pltpu.VMEM((NVAR, 128), F32), pltpu.VMEM((96, 128), F32),
         pltpu.VMEM((8, 128), F32), pltpu.SMEM((NY * NZ,), jnp.int32)],
        mib=BIG, flops=1 << 20, nbytes=2 << 20, name="slot_sum",
    )(*routing, got)
    main = lax.all_to_all(main, "z", 0, 0, tiled=True)
    both = jnp.concatenate([main.reshape(NZ * 96, 128), rest], axis=0)
    pieces = [both, send(both, "y", 1), send(both, "y", -1), send(both, "y", 2)]
    return call(
        spread_kernel, (sds((NVAR, PP, W), F32), sds((NVAR, W), F32), sds((1, W), F32)), 1, 4,
        [pltpu.VMEM((96, 128), F32)], mib=BIG, flops=1 << 20, nbytes=3 << 20, name="spread",
    )(info, both, *map(hbm, pieces[1:]))


def mix_kernel(agg_ref, own, p1, p2, out_ref):
    total = agg_ref[:NP, :].astype(F32)
    for p in (own, p1, p2):
        total = total + p[...].astype(F32)
    out_ref[0] = total.astype(BF)


def pixel_gather(own):
    mine = jnp.stack([own, send(own, "x", 1), send(own, "x", -1), send(own, "x", 2)])
    return mine, send(mine, "c", 1)


def local(pixels, counts, var_ids, destination, embed_weight, var_embed, agg_query, ln_gain, fc_up, fc_down, cotangent):
    y, z, x, c = (lax.axis_index(a) for a in ("y", "z", "x", "c"))
    info = jnp.stack([y, z, x, c]).astype(jnp.int32)
    routing = destination, counts, var_ids.reshape(-1)
    g_own = cotangent[0]
    down = lax.all_gather(fc_down, ("y", "z"), axis=0, tiled=True)

    to_rank = destination[None, :] == jnp.arange(NY * NZ)[:, None]
    ordered = dot(to_rank.astype(BF), pixels[:, 0, :]).astype(BF)
    mine = lax.all_to_all(ordered, ("y", "z"), 0, 0, tiled=True)
    q, info, mine = lax.optimization_barrier((agg_query.reshape(1, W), info, mine))
    mine, swapped = pixel_gather(mine)

    agg, emb, attn, patches = attention_forward(info, routing, (mine, swapped), embed_weight, var_embed, q, ln_gain)
    pieces = tensor_gather(agg)
    pre, dg, hid, u, st = up_call(info, pieces, fc_up)
    g_late, _ = lax.optimization_barrier((g_own, u))
    g_pieces = tensor_gather(g_late)
    up_src, _ = lax.optimization_barrier((fc_up, g_pieces[4]))
    up_kept = keep(up_src)
    rows = call(rows_kernel, sds((256, NP), BF), 0, 1, mib=BIG, nbytes=1 << 20, name="rows")(patches)
    down, up_kept, g_whole, rows = lax.optimization_barrier((down, up_kept, join(info, g_pieces), rows))
    gp, sums = grad_pre(g_whole, down, pre, dg, u)
    gn = tensor_scatter(info, gp, up_kept, sums, "gn", True)
    mark, _ = lax.optimization_barrier((sums, gn[0]))
    hid, _ = lax.optimization_barrier((hid, send(mark, "c", 1)))
    br = tensor_scatter(info, hid, down, None, "br", False)
    outs = attention_backward(gn, agg, st, ln_gain, g_own, emb, attn, rows, q)
    mixed = call(mix_kernel, sds((1, NP, W), BF), 0, 4, mib=BIG, nbytes=1 << 20, name="mix")(
        agg, br[0], *map(hbm, br[1:]))
    ge, gv, gq = gradient_exchange(info, routing, outs)
    return mixed, ge, gv, gq.reshape(W)


def solution(mesh):
    fine = Mesh(mesh.devices.reshape(NY, NZ, NX, NC), ("y", "z", "x", "c"))
    dp, tensor = ("y", "z"), ("x", "c")
    in_specs = (
        P(None, dp + tensor, None), P(), P(), P(), P(None, None, tensor), P(None, tensor), P(tensor),
        P(None, tensor), P(None, tensor), P(dp, tensor), P(dp, None, tensor),
    )
    out_specs = (P(dp, None, tensor), P(None, None, tensor), P(None, tensor), P(tensor))
    return jax.shard_map(local, mesh=fine, in_specs=in_specs, out_specs=out_specs, check_vma=False)
```

```python
import functools

import jax
import jax.numpy as jnp
from jax import lax
from jax.experimental import pallas as pl
from jax.experimental.pallas import tpu as pltpu
from jax.sharding import Mesh, PartitionSpec as P

HEAD = 128
VMAX = 8
PP = 16
NVAR = 48
D = 4096
FF = 8192
NP = 256
W = 512
HID = 1024
EXT = NP + 16
BF = jnp.bfloat16
F32 = jnp.float32
NT = (((1,), (1,)), ((), ()))
VM = pl.BlockSpec(memory_space=pltpu.VMEM)
SM = pl.BlockSpec(memory_space=pltpu.SMEM)
NX, NY, NZ, NC = 4, 4, 8, 2
BIG = 16


def params(mib):
    return pltpu.CompilerParams(vmem_limit_bytes=mib << 20)


def call(kernel, outs, n_smem, n_vmem, scratch=(), mib=BIG, flops=0, nbytes=0, name=None):
    single = not isinstance(outs, (list, tuple))
    return pl.pallas_call(
        kernel,
        out_shape=outs if single else tuple(outs),
        in_specs=[SM] * n_smem + [VM] * n_vmem,
        out_specs=VM if single else tuple([VM] * len(outs)),
        scratch_shapes=list(scratch),
        compiler_params=params(mib),
        cost_estimate=pl.CostEstimate(flops=flops, bytes_accessed=nbytes, transcendentals=0),
        name=name,
    )


def sds(shape, dtype):
    return jax.ShapeDtypeStruct(shape, dtype)


def hbm(a):
    return pltpu.with_memory_space_constraint(a, pltpu.HBM)


def send(a, axis, k):
    n = {"x": NX, "y": NY, "z": NZ, "c": NC}[axis]
    return lax.ppermute(a, axis, [(i, (i + k) % n) for i in range(n)])


def around(a, axis):
    n = {"x": NX, "y": NY, "z": NZ}[axis]
    steps = [(2 * i + k, 2 * ((i + 1 - 2 * k) % n) + k) for i in range(n) for k in range(NC)]
    return lax.ppermute(a, (axis, "c"), steps)


def dot(a, b, dims=(((1,), (0,)), ((), ()))):
    return lax.dot_general(a, b, dims, preferred_element_type=F32)


def lane_group(shape):
    return lax.broadcasted_iota(jnp.int32, shape, 1) // 16


def head_mask(dtype):
    row = lax.broadcasted_iota(jnp.int32, (128, W), 0)
    col = lax.broadcasted_iota(jnp.int32, (128, W), 1)
    return jnp.where(row % 16 == col // HEAD, 1.0, 0.0).astype(dtype)


def over_slots(op, a):
    for shift in (16, 32, 64):
        a = op(a, pltpu.roll(a, shift, 1))
    return a


def find(destination, rank):
    return lax.fori_loop(0, NY * NZ, lambda i, s: jnp.where(destination[i] == rank, i, s), 0)


def fwd_kernel(info, destination, counts, var_ids, xa_ref, xb_ref, ew_ref, ve_ref, q_ref, gain_ref,
               agg_ref, emb_ref, attn_ref, x_ref, wblk, wsem):
    copies = []
    sample = find(destination, info[0] * NZ + info[1])
    count = counts[sample]
    ids = [var_ids[sample * VMAX + j] for j in range(VMAX)]
    for j in range(VMAX):
        copies.append(pltpu.make_async_copy(ew_ref.at[ids[j]], wblk.at[j, pl.ds(16 * j, 16), :], wsem.at[j]))
    zero = jnp.zeros((16, W), BF)
    for j in range(VMAX):
        for k in range(VMAX):
            if k != j:
                wblk[j, 16 * k:16 * (k + 1), :] = zero
    for cp in copies:
        cp.start()
    col = lax.broadcasted_iota(jnp.int32, (1, NP), 1)
    device = jnp.zeros((1, NP), jnp.int32)
    for k in range(8):
        chip, core = (info[2] + (0, 3, 1, 2)[k % 4]) % 4, (info[3] + k // 4) % 2
        device = jnp.where(col // 32 == k, 2 * chip + core, device)
    row = lax.broadcasted_iota(jnp.int32, (NP, NP), 0)
    order = jnp.where(row == 8 * (col % 32) + device, 1.0, 0.0).astype(BF)
    pieces = jnp.concatenate([r[k] for r in (xa_ref, xb_ref) for k in range(4)], axis=0)
    x_ref[...] = dot(order, pieces).astype(BF)
    at_slot = lax.broadcasted_iota(jnp.int32, (16, NVAR), 0)
    at_var = lax.broadcasted_iota(jnp.int32, (16, NVAR), 1)
    onehot = jnp.zeros((16, NVAR), F32)
    for j in range(VMAX):
        onehot = jnp.where((at_slot == j) & (at_var == ids[j]), 1.0, onehot)
    bias = dot(onehot.astype(BF), ve_ref[...])
    expand = head_mask(BF)
    qmat = (expand.astype(F32) * q_ref[...].astype(F32)).astype(BF)
    for cp in copies:
        cp.wait()
    rows = 128
    group = lane_group((rows, 128))
    for r in range(NP // rows):
        at = slice(r * rows, (r + 1) * rows)
        x = x_ref[at, :]
        scores = jnp.zeros((rows, 128), F32)
        for j in range(VMAX):
            e = (dot(x, wblk[j]) + bias[j:j + 1, :]).astype(BF)
            emb_ref[j, at, :] = e
            scores = jnp.where(group == j, dot(e, qmat, NT), scores)
        scores = scores * (HEAD ** -0.5)
        scores = jnp.where(group < count, scores, -jnp.inf)
        top = over_slots(jnp.maximum, scores)
        raised = jnp.exp(scores - top)
        attn = raised / over_slots(jnp.add, raised)
        attn_ref[at, :] = attn
        attn_b = attn.astype(BF)
        total = jnp.zeros((rows, W), F32)
        for j in range(VMAX):
            wide = dot(jnp.where(group == j, attn_b, jnp.zeros_like(attn_b)), expand)
            total = total + wide * emb_ref[j, at, :].astype(F32)
        agg_ref[at, :] = total.astype(BF)
    agg_ref[NP:EXT, :] = jnp.broadcast_to(gain_ref[...], (16, W))


def attention_forward(info, routing, xs, ew, ve, q, gain):
    return pl.pallas_call(
        fwd_kernel,
        out_shape=(sds((EXT, W), BF), sds((VMAX, NP, W), BF), sds((NP, 128), F32), sds((NP, 128), BF)),
        in_specs=[SM] * 4 + [VM, VM, pl.BlockSpec(memory_space=pl.ANY), VM, VM, VM],
        out_specs=(VM, VM, VM, VM),
        scratch_shapes=[pltpu.VMEM((VMAX, 128, W), BF), pltpu.SemaphoreType.DMA((VMAX,))],
        compiler_params=params(BIG),
        cost_estimate=pl.CostEstimate(flops=2 * 3 * 8 * 256 * 128 * 512, bytes_accessed=4 << 20, transcendentals=0),
        name="attn_fwd",
    )(info, *routing, *xs, ew, ve, q, gain)


def tensor_gather(a):
    first = around(a, "x")
    other = send(a, "c", 1)
    second = around(other, "x")
    far = around(first, "x")
    return a, other, first, second, far, send(first, "c", 1), send(second, "c", 1), send(far, "c", 1)


def blocks_of(info, refs):
    x, c = info[2], info[3]
    d = 1 - 2 * c
    back, fore, opposite = (x + 4 - d) % 4, (x + 4 + d) % 4, (x + 2) % 4
    place = ((x, c), (x, 1 - c), (back, c), (back, 1 - c), (opposite, c), (fore, 1 - c), (fore, c), (opposite, 1 - c))
    return [(chip, core, ref) for (chip, core), ref in zip(place, refs)]


def up_kernel(info, *refs):
    pieces, up_ref = refs[:8], refs[8]
    pre_ref, dg_ref, hid_ref, u_ref, st_ref, nrm = refs[9:]

    @pl.when(pl.program_id(0) == 0)
    def _():
        blocks = [(2 * chip + core, p) for chip, core, p in blocks_of(info, pieces)]
        for r in range(4):
            lo, hi = 64 * r, 64 * r + 64
            total = jnp.zeros((64, W), F32)
            for _, p in blocks:
                total = total + p[lo:hi, :].astype(F32)
            mean = jnp.sum(total, axis=1, keepdims=True) * (1.0 / D)
            total = jnp.zeros((64, W), F32)
            for _, p in blocks:
                d = p[lo:hi, :].astype(F32) - mean
                total = total + d * d
            inv = lax.rsqrt(jnp.sum(total, axis=1, keepdims=True) * (1.0 / D) + 1e-05)
            st_ref[0, lo:hi, :] = jnp.broadcast_to(mean, (64, 128))
            st_ref[1, lo:hi, :] = jnp.broadcast_to(inv, (64, 128))
            for b, p in blocks:
                gain = p[NP:EXT, :][0:1, :].astype(F32)
                col = pl.ds(pl.multiple_of(b * W, W), W)
                nrm[lo:hi, col] = ((p[lo:hi, :].astype(F32) - mean) * inv * gain).astype(BF)
        for b, p in blocks:
            nrm[NP:EXT, pl.ds(pl.multiple_of(b * W, W), W)] = p[NP:EXT, :]

    acc = dot(nrm[...], up_ref[...])
    x = acc[:NP]
    c = 0.7978845608028654
    th = jnp.tanh(c * (x + 0.044715 * (x * x * x)))
    pre_ref[...] = x
    hid_ref[...] = (0.5 * x * (1.0 + th)).astype(BF)
    dg_ref[...] = 0.5 * (1.0 + th) + 0.5 * x * (1.0 - th * th) * (c * (1.0 + 3 * 0.044715 * (x * x)))
    u_ref[...] = acc[NP:NP + 8]


def up_call(info, pieces, fc_up):
    n = 4
    w = HID // n
    whole = [pl.BlockSpec(p.shape, lambda i: (0, 0)) for p in pieces]
    return pl.pallas_call(
        up_kernel,
        grid=(n,),
        out_shape=(sds((NP, HID), F32), sds((NP, HID), F32), sds((NP, HID), BF), sds((8, HID), F32), sds((2, NP, 128), F32)),
        in_specs=[SM] + whole + [pl.BlockSpec((D, w), lambda i: (0, i))],
        out_specs=(
            pl.BlockSpec((NP, w), lambda i: (0, i)), pl.BlockSpec((NP, w), lambda i: (0, i)),
            pl.BlockSpec((NP, w), lambda i: (0, i)), pl.BlockSpec((8, w), lambda i: (0, i)),
            pl.BlockSpec((2, NP, 128), lambda i: (0, 0, 0)),
        ),
        scratch_shapes=[pltpu.VMEM((EXT, D), BF)],
        compiler_params=params(BIG),
        cost_estimate=pl.CostEstimate(flops=2 * EXT * D * HID, bytes_accessed=16 << 20, transcendentals=0),
        name="ln_up",
    )(info, *map(hbm, pieces), hbm(fc_up))


def split3(row):
    hi = row.astype(BF).astype(F32)
    mid = (row - hi).astype(BF).astype(F32)
    return hi, mid, row - hi - mid


def ride(row):
    hi, mid, low = split3(row)
    at = lax.broadcasted_iota(jnp.int32, (16, W), 0)
    tile = jnp.where(at == 0, hi, jnp.where(at == 1, mid, jnp.where(at == 2, low, 0.0)))
    return tile.astype(BF)


def unride(tile):
    return jnp.sum(tile.astype(F32), axis=0, keepdims=True)


def join_kernel(info, *refs):
    pieces, out = refs[:8], refs[8]
    for chip, core, p in blocks_of(info, pieces):
        out[:, pl.ds(pl.multiple_of((2 * chip + core) * W, W), W)] = p[...]


def join(info, pieces):
    return call(join_kernel, sds((NP, D), BF), 1, 8, mib=BIG, nbytes=4 << 20, name="join")(info, *map(hbm, pieces))


def gh_kernel(g, down_ref, pre_ref, dg_ref, u_ref, gp_ref, s_ref, tot):
    i = pl.program_id(0)

    @pl.when(i == 0)
    def _():
        tot[...] = jnp.zeros_like(tot)

    gh = dot(g[...], down_ref[...])
    gp = (gh * dg_ref[...]).astype(BF)
    gp_ref[...] = gp
    gpf = gp.astype(F32)
    a = gpf * u_ref[0:1, :]
    b = gpf * pre_ref[...]
    for k, p in enumerate((a, b)):
        tot[k] += sum(p[:, 128 * m:128 * m + 128] for m in range(p.shape[1] // 128))

    @pl.when(i == pl.num_programs(0) - 1)
    def _():
        s_ref[...] = ride(sums_row(tot[0], tot[1]))


def grad_pre(g, down, pre, dg, u):
    n = 2
    w = HID // n

    def col(r):
        return pl.BlockSpec((r, w), lambda i: (0, i))

    return pl.pallas_call(
        gh_kernel,
        grid=(n,),
        out_shape=(sds((NP, HID), BF), sds((16, W), BF)),
        in_specs=[VM, col(D), col(NP), col(NP), col(8)],
        out_specs=(col(NP), pl.BlockSpec((16, W), lambda i: (0, 0))),
        scratch_shapes=[pltpu.VMEM((2, NP, 128), F32)],
        compiler_params=params(24),
        cost_estimate=pl.CostEstimate(flops=2 * NP * D * HID, bytes_accessed=12 << 20, transcendentals=0),
        name="grad_pre",
    )(g, hbm(down), hbm(pre), hbm(dg), u)


def sums_row(a, b):
    rows = []
    for t in (a, b):
        s = jnp.broadcast_to(jnp.sum(t, axis=1, keepdims=True), (NP, 128))
        rows.append(jnp.transpose(s)[0:1, :])
    return jnp.concatenate(rows, axis=1)


def keep_kernel(src, dst, sem):
    copy = pltpu.make_async_copy(src, dst, sem)
    copy.start()
    copy.wait()


def keep(a):
    return pl.pallas_call(
        keep_kernel,
        out_shape=pltpu.VMEM(a.shape, a.dtype),
        in_specs=[pl.BlockSpec(memory_space=pltpu.HBM)],
        out_specs=pl.BlockSpec(memory_space=pltpu.VMEM),
        scratch_shapes=[pltpu.SemaphoreType.DMA],
        compiler_params=params(12),
        cost_estimate=pl.CostEstimate(flops=0, bytes_accessed=2 * a.size * 2, transcendentals=0),
        name="keep",
    )(a)


def nt_kernel(steps, other, kept, with_sums, first_add, stacked, info, lhs_ref, rhs_ref, *refs):
    refs = list(refs)
    s_ref = refs.pop(0) if with_sums else None
    add_ref = refs.pop(0) if first_add is not None else None
    core = 1 - info[3] if other else info[3]
    n = len(steps)
    rows = [pl.ds(pl.multiple_of((2 * ((info[2] + k) % NX) + core) * W, W), W) for k in steps]
    if not kept:
        buf, sem = refs[-2:]
        copies = [pltpu.make_async_copy(rhs_ref.at[rows[i], :], buf.at[i], sem.at[i]) for i in range(n)]
        for cp in copies:
            cp.start()
    for i in range(n):
        if not kept:
            copies[i].wait()
        out = refs[0].at[i] if stacked else refs[i]
        acc = dot(lhs_ref[...], rhs_ref[rows[i], :] if kept else buf[i], NT)
        if first_add is not None:
            acc = acc + add_ref[first_add + i, :NP, :].astype(F32)
        out[:NP, :] = acc.astype(BF)
        if with_sums:
            if first_add is not None:
                out[NP:, :] = ride(unride(s_ref[...]) + unride(add_ref[first_add + i, NP:, :]))
            else:
                out[NP:, :] = s_ref[...]


def nt_call(steps, other, kept, info, lhs, rhs, sums=None, add=None, first_add=None, stacked=False, name=None):
    n = len(steps)
    rows = EXT if sums is not None else NP
    args = [info, lhs, rhs if kept else hbm(rhs)]
    in_specs = [SM, VM, VM if kept else pl.BlockSpec(memory_space=pltpu.HBM)]
    for extra in (sums, add):
        if extra is not None:
            args.append(extra)
            in_specs.append(VM)
    return pl.pallas_call(
        functools.partial(nt_kernel, steps, other, kept, sums is not None, first_add, stacked),
        in_specs=in_specs,
        out_specs=VM if stacked else tuple([VM] * n),
        out_shape=sds((n, rows, W), BF) if stacked else tuple([sds((rows, W), BF)] * n),
        scratch_shapes=[] if kept else [pltpu.VMEM((n, W, HID), BF), pltpu.SemaphoreType.DMA((n,))],
        compiler_params=params(BIG),
        cost_estimate=pl.CostEstimate(flops=2 * NP * HID * W * n, bytes_accessed=n << 20, transcendentals=0),
        name=name,
    )(*args)


def half_kernel(a_ref, b_ref, out_ref):
    out_ref[:NP, :] = a_ref[:NP, :].astype(F32) + b_ref[:NP, :].astype(F32)
    if a_ref.shape[0] > NP:
        at = lax.broadcasted_iota(jnp.int32, (16, W), 0)
        out_ref[NP:, :] = jnp.where(at == 0, unride(a_ref[NP:, :]) + unride(b_ref[NP:, :]), 0.0)


def tensor_scatter(info, lhs, rhs, sums, name, kept):
    o = send(nt_call((2, 1, 3, 0), True, kept, info, lhs, rhs, sums, stacked=True, name=name + "_o"), "c", 1)
    far, = nt_call((2,), False, kept, info, lhs, rhs, sums, o, 0, name=name + "_f")
    lhs, far = lax.optimization_barrier((lhs, far))
    far = send(far, "x", 2)
    ahead, behind, own = nt_call((1, 3, 0), False, kept, info, lhs, rhs, sums, o, 1, name=name + "_n")
    return call(half_kernel, sds(own.shape, F32), 0, 2, mib=BIG, nbytes=1 << 20, name=name + "_p")(own, far), send(
        ahead, "x", 1), send(behind, "x", -1)


def rows_kernel(x_ref, out_ref):
    row = lax.broadcasted_iota(jnp.int32, (256, 128), 0)
    col = lax.broadcasted_iota(jnp.int32, (256, 128), 1)
    pixel = 16 * (row // 32) + 2 * (row % 32 // 4) + row % 4
    chosen = jnp.where((col == pixel) & (row % 4 < 2), 1.0, 0.0).astype(BF)
    got = dot(chosen, x_ref[...], NT)
    at = lax.broadcasted_iota(jnp.int32, (256, NP), 0)
    out_ref[...] = jnp.where(at % 4 < 2, got, 1.0).astype(BF)


def bwd_kernel(own_ref, p1_ref, p2_ref, agg_ref, st_ref, gain_ref, g_ref, emb_ref, attn_ref, x_ref, q_ref,
               *rest):
    out_ref, acc, gq = rest
    parts = (own_ref, p1_ref, p2_ref)
    expand = head_mask(BF)
    scale = HEAD ** -0.5
    qrow = q_ref[...].astype(F32) * scale
    gain = gain_ref[...].astype(F32)
    sums = sum(unride(p[NP:, :]) for p in parts)
    cols = []
    for k in range(2):
        row = sums[:, k * NP:(k + 1) * NP] * (1.0 / D)
        cols.append(jnp.transpose(jnp.broadcast_to(row, (128, NP))))
    expand2 = jnp.concatenate([expand, expand], axis=0)
    rows = NP
    group = lane_group((rows, 128))
    group2 = lax.broadcasted_iota(jnp.int32, (rows, 256), 1) % 128 // 16
    for r in range(NP // rows):
        at = slice(r * rows, (r + 1) * rows)
        mean, inv = st_ref[0, at, 0:1], st_ref[1, at, 0:1]
        xh = (agg_ref[at, :].astype(F32) - mean) * inv
        gs = sum(p[at, :].astype(F32) for p in parts) * gain
        ga = g_ref[at, :].astype(F32) + inv * (gs - cols[0][at, 0:1] - xh * cols[1][at, 0:1])
        gab = ga.astype(BF).astype(F32)
        gattn = jnp.zeros((rows, 128), F32)
        for j in range(VMAX):
            prod = gab * emb_ref[j, at, :].astype(F32)
            hi = prod.astype(BF)
            low = (prod - hi.astype(F32)).astype(BF)
            both = dot(hi, expand, NT) + dot(low, expand, NT)
            gattn = jnp.where(group == j, both, gattn)
        attn = attn_ref[at, :]
        gscore = attn * (gattn - over_slots(jnp.add, attn * gattn))
        ahi = attn.astype(BF)
        alow = (attn - ahi.astype(F32)).astype(BF)
        shi = gscore.astype(BF)
        slow = (gscore - shi.astype(F32)).astype(BF)
        a2 = jnp.concatenate([ahi, alow], axis=1)
        s2 = jnp.concatenate([shi, slow], axis=1)
        zero = jnp.zeros_like(a2)
        gst = jnp.transpose(shi.astype(F32)).astype(BF)
        for j in range(VMAX):
            pick = group2 == j
            a_w = dot(jnp.where(pick, a2, zero), expand2)
            s_w = dot(jnp.where(pick, s2, zero), expand2)
            ge = (a_w * ga + s_w * qrow).astype(BF)
            mine = slice(16 * j, 16 * j + 16)
            part_q = dot(gst[mine, :], emb_ref[j, at, :])
            gq[mine, :] = part_q if r == 0 else gq[mine, :] + part_q
            got = dot(x_ref[32 * j:32 * j + 32, at], ge)
            for z in range(NZ):
                to = slice(32 * z + 4 * j, 32 * z + 4 * j + 4)
                if r == 0:
                    acc[to, :] = got[4 * z:4 * z + 4]
                else:
                    acc[to, :] += got[4 * z:4 * z + 4]
    total_q = jnp.sum(gq[...] * expand.astype(F32), axis=0, keepdims=True) * scale
    for z in range(NZ):
        acc[32 * z + 3:32 * z + 4, :] = total_q
        for y in range(NY):
            out_ref[NZ * y + z] = acc[32 * z:32 * z + 32, 128 * y:128 * y + 128].astype(BF)


def attention_backward(gn, agg, st, gain, g, emb, attn, x, q):
    return call(
        bwd_kernel, sds((NY * NZ, 32, 128), BF), 0, 11, [pltpu.VMEM((256, W), F32), pltpu.VMEM((128, W), F32)], mib=BIG,
        flops=2 * 6 * 8 * 256 * 128 * 512, nbytes=5 << 20, name="attn_bwd",
    )(gn[0], *map(hbm, gn[1:]), agg, st, gain, hbm(g), emb, attn, x, q)


def sum_kernel(destination, counts, ids, got_ref, main_ref, rest_ref, acc, bias, pair, query, inverse):
    acc[...] = jnp.zeros_like(acc)
    for i in range(NY * NZ):
        inverse[destination[i]] = i
    total = jnp.zeros((8, 128), F32)
    for rank in range(NY * NZ):
        sample = inverse[rank]
        live = counts[sample]
        data = got_ref[rank].astype(F32)
        total = total + data[0:8]
        for j in range(VMAX):
            v = jnp.where(j < live, ids[sample * VMAX + j], NVAR)
            acc[v, 0:4, :] += data[4 * j:4 * j + 4]
    query[...] = total
    for v in range(NVAR):
        pair[2 * v:2 * v + 2, :] = acc[v, 0:2, :]
        bias[v:v + 1, :] = acc[v, 2:3, :]
    for z in range(NZ):
        main_ref[z] = pair[...].astype(BF)
    rest_ref[0:48, :] = bias[...].astype(BF)
    rest_ref[48:64, :] = jnp.broadcast_to(query[3:4, :], (16, 128)).astype(BF)


def spread_kernel(info, *refs):
    pieces = refs[0:4]
    ge_ref, gv_ref, gq_ref, pair = refs[4:]
    for k, piece in enumerate(pieces):
        col = pl.ds(pl.multiple_of((info[0] + (0, 3, 1, 2)[k]) % NY * 128, 128), 128)
        for z in range(NZ):
            pair[...] = piece[96 * z:96 * z + 96, :].astype(F32)
            for v in range(NVAR):
                ge_ref[v, 2 * z:2 * z + 2, col] = pair[2 * v:2 * v + 2, :]
        gv_ref[:, col] = piece[768:816, :].astype(F32)
        gq_ref[:, col] = piece[816:832, :].astype(F32)[0:1]


def gradient_exchange(info, routing, outs):
    got = lax.all_to_all(outs, ("y", "z"), 0, 0, tiled=True)
    main, rest = call(
        sum_kernel, (sds((NZ, 96, 128), BF), sds((64, 128), BF)), 3, 1,
        [pltpu.VMEM((NVAR + 1, 8, 128), F32), pltpu.VMEM((NVAR, 128), F32), pltpu.VMEM((96, 128), F32),
         pltpu.VMEM((8, 128), F32), pltpu.SMEM((NY * NZ,), jnp.int32)],
        mib=BIG, flops=1 << 20, nbytes=2 << 20, name="slot_sum",
    )(*routing, got)
    main = lax.all_to_all(main, "z", 0, 0, tiled=True)
    both = jnp.concatenate([main.reshape(NZ * 96, 128), rest], axis=0)
    pieces = [both, send(both, "y", 1), send(both, "y", -1), send(both, "y", 2)]
    return call(
        spread_kernel, (sds((NVAR, PP, W), F32), sds((NVAR, W), F32), sds((1, W), F32)), 1, 4,
        [pltpu.VMEM((96, 128), F32)], mib=BIG, flops=1 << 20, nbytes=3 << 20, name="spread",
    )(info, both, *map(hbm, pieces[1:]))


def mix_kernel(agg_ref, own, p1, p2, out_ref):
    total = agg_ref[:NP, :].astype(F32)
    for p in (own, p1, p2):
        total = total + p[...].astype(F32)
    out_ref[0] = total.astype(BF)


def pixel_gather(own):
    mine = jnp.stack([own, send(own, "x", 1), send(own, "x", -1), send(own, "x", 2)])
    return mine, send(mine, "c", 1)


def local(pixels, counts, var_ids, destination, embed_weight, var_embed, agg_query, ln_gain, fc_up, fc_down, cotangent):
    y, z, x, c = (lax.axis_index(a) for a in ("y", "z", "x", "c"))
    info = jnp.stack([y, z, x, c]).astype(jnp.int32)
    routing = destination, counts, var_ids.reshape(-1)
    g_own = cotangent[0]
    down = lax.all_gather(fc_down, ("y", "z"), axis=0, tiled=True)

    to_rank = destination[None, :] == jnp.arange(NY * NZ)[:, None]
    ordered = dot(to_rank.astype(BF), pixels[:, 0, :]).astype(BF)
    mine = lax.all_to_all(ordered, ("y", "z"), 0, 0, tiled=True)
    q, info, mine = lax.optimization_barrier((agg_query.reshape(1, W), info, mine))
    mine, swapped = pixel_gather(mine)

    agg, emb, attn, patches = attention_forward(info, routing, (mine, swapped), embed_weight, var_embed, q, ln_gain)
    pieces = tensor_gather(agg)
    pre, dg, hid, u, st = up_call(info, pieces, fc_up)
    g_late, _ = lax.optimization_barrier((g_own, u))
    g_pieces = tensor_gather(g_late)
    up_src, _ = lax.optimization_barrier((fc_up, g_pieces[4]))
    up_kept = keep(up_src)
    rows = call(rows_kernel, sds((256, NP), BF), 0, 1, mib=BIG, nbytes=1 << 20, name="rows")(patches)
    down, up_kept, g_whole, rows = lax.optimization_barrier((down, up_kept, join(info, g_pieces), rows))
    gp, sums = grad_pre(g_whole, down, pre, dg, u)
    gn = tensor_scatter(info, gp, up_kept, sums, "gn", True)
    mark, _ = lax.optimization_barrier((sums, gn[0]))
    hid, _ = lax.optimization_barrier((hid, send(mark, "c", 1)))
    br = tensor_scatter(info, hid, down, None, "br", False)
    outs = attention_backward(gn, agg, st, ln_gain, g_own, emb, attn, rows, q)
    mixed = call(mix_kernel, sds((1, NP, W), BF), 0, 4, mib=BIG, nbytes=1 << 20, name="mix")(
        agg, br[0], *map(hbm, br[1:]))
    ge, gv, gq = gradient_exchange(info, routing, outs)
    return mixed, ge, gv, gq.reshape(W)


def solution(mesh):
    fine = Mesh(mesh.devices.reshape(NY, NZ, NX, NC), ("y", "z", "x", "c"))
    dp, tensor = ("y", "z"), ("x", "c")
    in_specs = (
        P(None, dp + tensor, None), P(), P(), P(), P(None, None, tensor), P(None, tensor), P(tensor),
        P(None, tensor), P(None, tensor), P(dp, tensor), P(dp, None, tensor),
    )
    out_specs = (P(dp, None, tensor), P(None, None, tensor), P(None, tensor), P(tensor))
    return jax.shard_map(local, mesh=fine, in_specs=in_specs, out_specs=out_specs, check_vma=False)
```

```python
import functools

import jax
import jax.numpy as jnp
from jax import lax
from jax.experimental import pallas as pl
from jax.experimental.pallas import tpu as pltpu
from jax.sharding import Mesh, PartitionSpec as P

HEAD = 128
VMAX = 8
PP = 16
NVAR = 48
D = 4096
FF = 8192
NP = 256
W = 512
HID = 1024
EXT = NP + 16
BF = jnp.bfloat16
F32 = jnp.float32
NT = (((1,), (1,)), ((), ()))
VM = pl.BlockSpec(memory_space=pltpu.VMEM)
SM = pl.BlockSpec(memory_space=pltpu.SMEM)
NX, NY, NZ, NC = 4, 4, 8, 2
BIG = 16


def params(mib):
    return pltpu.CompilerParams(vmem_limit_bytes=mib << 20)


def call(kernel, outs, n_smem, n_vmem, scratch=(), mib=BIG, flops=0, nbytes=0, name=None):
    single = not isinstance(outs, (list, tuple))
    return pl.pallas_call(
        kernel,
        out_shape=outs if single else tuple(outs),
        in_specs=[SM] * n_smem + [VM] * n_vmem,
        out_specs=VM if single else tuple([VM] * len(outs)),
        scratch_shapes=list(scratch),
        compiler_params=params(mib),
        cost_estimate=pl.CostEstimate(flops=flops, bytes_accessed=nbytes, transcendentals=0),
        name=name,
    )


def sds(shape, dtype):
    return jax.ShapeDtypeStruct(shape, dtype)


def hbm(a):
    return pltpu.with_memory_space_constraint(a, pltpu.HBM)


def send(a, axis, k):
    n = {"x": NX, "y": NY, "z": NZ, "c": NC}[axis]
    return lax.ppermute(a, axis, [(i, (i + k) % n) for i in range(n)])


def around(a, axis):
    n = {"x": NX, "y": NY, "z": NZ}[axis]
    steps = [(2 * i + k, 2 * ((i + 1 - 2 * k) % n) + k) for i in range(n) for k in range(NC)]
    return lax.ppermute(a, (axis, "c"), steps)


def dot(a, b, dims=(((1,), (0,)), ((), ()))):
    return lax.dot_general(a, b, dims, preferred_element_type=F32)


def lane_group(shape):
    return lax.broadcasted_iota(jnp.int32, shape, 1) // 16


def head_mask(dtype):
    row = lax.broadcasted_iota(jnp.int32, (128, W), 0)
    col = lax.broadcasted_iota(jnp.int32, (128, W), 1)
    return jnp.where(row % 16 == col // HEAD, 1.0, 0.0).astype(dtype)


def over_slots(op, a):
    for shift in (16, 32, 64):
        a = op(a, pltpu.roll(a, shift, 1))
    return a


def find(destination, rank):
    return lax.fori_loop(0, NY * NZ, lambda i, s: jnp.where(destination[i] == rank, i, s), 0)


def fwd_kernel(info, destination, counts, var_ids, xa_ref, xb_ref, ew_ref, ve_ref, q_ref, gain_ref,
               agg_ref, emb_ref, attn_ref, x_ref, wblk, wsem):
    copies = []
    sample = find(destination, info[0] * NZ + info[1])
    count = counts[sample]
    ids = [var_ids[sample * VMAX + j] for j in range(VMAX)]
    for j in range(VMAX):
        copies.append(pltpu.make_async_copy(ew_ref.at[ids[j]], wblk.at[j, pl.ds(16 * j, 16), :], wsem.at[j]))
    zero = jnp.zeros((16, W), BF)
    for j in range(VMAX):
        for k in range(VMAX):
            if k != j:
                wblk[j, 16 * k:16 * (k + 1), :] = zero
    for cp in copies:
        cp.start()
    col = lax.broadcasted_iota(jnp.int32, (1, NP), 1)
    device = jnp.zeros((1, NP), jnp.int32)
    for k in range(8):
        chip, core = (info[2] + (0, 3, 1, 2)[k % 4]) % 4, (info[3] + k // 4) % 2
        device = jnp.where(col // 32 == k, 2 * chip + core, device)
    row = lax.broadcasted_iota(jnp.int32, (NP, NP), 0)
    order = jnp.where(row == 8 * (col % 32) + device, 1.0, 0.0).astype(BF)
    pieces = jnp.concatenate([r[k] for r in (xa_ref, xb_ref) for k in range(4)], axis=0)
    x_ref[...] = dot(order, pieces).astype(BF)
    at_slot = lax.broadcasted_iota(jnp.int32, (16, NVAR), 0)
    at_var = lax.broadcasted_iota(jnp.int32, (16, NVAR), 1)
    onehot = jnp.zeros((16, NVAR), F32)
    for j in range(VMAX):
        onehot = jnp.where((at_slot == j) & (at_var == ids[j]), 1.0, onehot)
    bias = dot(onehot.astype(BF), ve_ref[...])
    expand = head_mask(BF)
    qmat = (expand.astype(F32) * q_ref[...].astype(F32)).astype(BF)
    for cp in copies:
        cp.wait()
    rows = 128
    group = lane_group((rows, 128))
    for r in range(NP // rows):
        at = slice(r * rows, (r + 1) * rows)
        x = x_ref[at, :]
        scores = jnp.zeros((rows, 128), F32)
        for j in range(VMAX):
            e = (dot(x, wblk[j]) + bias[j:j + 1, :]).astype(BF)
            emb_ref[j, at, :] = e
            scores = jnp.where(group == j, dot(e, qmat, NT), scores)
        scores = scores * (HEAD ** -0.5)
        scores = jnp.where(group < count, scores, -jnp.inf)
        top = over_slots(jnp.maximum, scores)
        raised = jnp.exp(scores - top)
        attn = raised / over_slots(jnp.add, raised)
        attn_ref[at, :] = attn
        attn_b = attn.astype(BF)
        total = jnp.zeros((rows, W), F32)
        for j in range(VMAX):
            wide = dot(jnp.where(group == j, attn_b, jnp.zeros_like(attn_b)), expand)
            total = total + wide * emb_ref[j, at, :].astype(F32)
        agg_ref[at, :] = total.astype(BF)
    agg_ref[NP:EXT, :] = jnp.broadcast_to(gain_ref[...], (16, W))


def attention_forward(info, routing, xs, ew, ve, q, gain):
    return pl.pallas_call(
        fwd_kernel,
        out_shape=(sds((EXT, W), BF), sds((VMAX, NP, W), BF), sds((NP, 128), F32), sds((NP, 128), BF)),
        in_specs=[SM] * 4 + [VM, VM, pl.BlockSpec(memory_space=pl.ANY), VM, VM, VM],
        out_specs=(VM, VM, VM, VM),
        scratch_shapes=[pltpu.VMEM((VMAX, 128, W), BF), pltpu.SemaphoreType.DMA((VMAX,))],
        compiler_params=params(BIG),
        cost_estimate=pl.CostEstimate(flops=2 * 3 * 8 * 256 * 128 * 512, bytes_accessed=4 << 20, transcendentals=0),
        name="attn_fwd",
    )(info, *routing, *xs, ew, ve, q, gain)


def tensor_gather(a):
    first = around(a, "x")
    other = send(a, "c", 1)
    second = around(other, "x")
    far = around(first, "x")
    return a, other, first, second, far, send(first, "c", 1), send(second, "c", 1), send(far, "c", 1)


def blocks_of(info, refs):
    x, c = info[2], info[3]
    d = 1 - 2 * c
    back, fore, opposite = (x + 4 - d) % 4, (x + 4 + d) % 4, (x + 2) % 4
    place = ((x, c), (x, 1 - c), (back, c), (back, 1 - c), (opposite, c), (fore, 1 - c), (fore, c), (opposite, 1 - c))
    return [(chip, core, ref) for (chip, core), ref in zip(place, refs)]


def up_kernel(info, *refs):
    pieces, up_ref = refs[:8], refs[8]
    pre_ref, dg_ref, hid_ref, u_ref, st_ref, nrm = refs[9:]

    @pl.when(pl.program_id(0) == 0)
    def _():
        blocks = [(2 * chip + core, p) for chip, core, p in blocks_of(info, pieces)]
        for r in range(4):
            lo, hi = 64 * r, 64 * r + 64
            total = jnp.zeros((64, W), F32)
            for _, p in blocks:
                total = total + p[lo:hi, :].astype(F32)
            mean = jnp.sum(total, axis=1, keepdims=True) * (1.0 / D)
            total = jnp.zeros((64, W), F32)
            for _, p in blocks:
                d = p[lo:hi, :].astype(F32) - mean
                total = total + d * d
            inv = lax.rsqrt(jnp.sum(total, axis=1, keepdims=True) * (1.0 / D) + 1e-05)
            st_ref[0, lo:hi, :] = jnp.broadcast_to(mean, (64, 128))
            st_ref[1, lo:hi, :] = jnp.broadcast_to(inv, (64, 128))
            for b, p in blocks:
                gain = p[NP:EXT, :][0:1, :].astype(F32)
                col = pl.ds(pl.multiple_of(b * W, W), W)
                nrm[lo:hi, col] = ((p[lo:hi, :].astype(F32) - mean) * inv * gain).astype(BF)
        for b, p in blocks:
            nrm[NP:EXT, pl.ds(pl.multiple_of(b * W, W), W)] = p[NP:EXT, :]

    acc = dot(nrm[...], up_ref[...])
    x = acc[:NP]
    c = 0.7978845608028654
    th = jnp.tanh(c * (x + 0.044715 * (x * x * x)))
    pre_ref[...] = x
    hid_ref[...] = (0.5 * x * (1.0 + th)).astype(BF)
    dg_ref[...] = 0.5 * (1.0 + th) + 0.5 * x * (1.0 - th * th) * (c * (1.0 + 3 * 0.044715 * (x * x)))
    u_ref[...] = acc[NP:NP + 8]


def up_call(info, pieces, fc_up):
    n = 4
    w = HID // n
    whole = [pl.BlockSpec(p.shape, lambda i: (0, 0)) for p in pieces]
    return pl.pallas_call(
        up_kernel,
        grid=(n,),
        out_shape=(sds((NP, HID), F32), sds((NP, HID), F32), sds((NP, HID), BF), sds((8, HID), F32), sds((2, NP, 128), F32)),
        in_specs=[SM] + whole + [pl.BlockSpec((D, w), lambda i: (0, i))],
        out_specs=(
            pl.BlockSpec((NP, w), lambda i: (0, i)), pl.BlockSpec((NP, w), lambda i: (0, i)),
            pl.BlockSpec((NP, w), lambda i: (0, i)), pl.BlockSpec((8, w), lambda i: (0, i)),
            pl.BlockSpec((2, NP, 128), lambda i: (0, 0, 0)),
        ),
        scratch_shapes=[pltpu.VMEM((EXT, D), BF)],
        compiler_params=params(BIG),
        cost_estimate=pl.CostEstimate(flops=2 * EXT * D * HID, bytes_accessed=16 << 20, transcendentals=0),
        name="ln_up",
    )(info, *map(hbm, pieces), hbm(fc_up))


def split3(row):
    hi = row.astype(BF).astype(F32)
    mid = (row - hi).astype(BF).astype(F32)
    return hi, mid, row - hi - mid


def ride(row):
    hi, mid, low = split3(row)
    at = lax.broadcasted_iota(jnp.int32, (16, W), 0)
    tile = jnp.where(at == 0, hi, jnp.where(at == 1, mid, jnp.where(at == 2, low, 0.0)))
    return tile.astype(BF)


def unride(tile):
    return jnp.sum(tile.astype(F32), axis=0, keepdims=True)


def join_kernel(info, *refs):
    pieces, out = refs[:8], refs[8]
    for chip, core, p in blocks_of(info, pieces):
        out[:, pl.ds(pl.multiple_of((2 * chip + core) * W, W), W)] = p[...]


def join(info, pieces):
    return call(join_kernel, sds((NP, D), BF), 1, 8, mib=BIG, nbytes=4 << 20, name="join")(info, *map(hbm, pieces))


def gh_kernel(g, down_ref, pre_ref, dg_ref, u_ref, gp_ref, s_ref, tot):
    i = pl.program_id(0)

    @pl.when(i == 0)
    def _():
        tot[...] = jnp.zeros_like(tot)

    gh = dot(g[...], down_ref[...])
    gp = (gh * dg_ref[...]).astype(BF)
    gp_ref[...] = gp
    gpf = gp.astype(F32)
    a = gpf * u_ref[0:1, :]
    b = gpf * pre_ref[...]
    for k, p in enumerate((a, b)):
        tot[k] += sum(p[:, 128 * m:128 * m + 128] for m in range(p.shape[1] // 128))

    @pl.when(i == pl.num_programs(0) - 1)
    def _():
        s_ref[...] = ride(sums_row(tot[0], tot[1]))


def grad_pre(g, down, pre, dg, u):
    n = 2
    w = HID // n

    def col(r):
        return pl.BlockSpec((r, w), lambda i: (0, i))

    return pl.pallas_call(
        gh_kernel,
        grid=(n,),
        out_shape=(sds((NP, HID), BF), sds((16, W), BF)),
        in_specs=[VM, col(D), col(NP), col(NP), col(8)],
        out_specs=(col(NP), pl.BlockSpec((16, W), lambda i: (0, 0))),
        scratch_shapes=[pltpu.VMEM((2, NP, 128), F32)],
        compiler_params=params(24),
        cost_estimate=pl.CostEstimate(flops=2 * NP * D * HID, bytes_accessed=12 << 20, transcendentals=0),
        name="grad_pre",
    )(g, hbm(down), hbm(pre), hbm(dg), u)


def sums_row(a, b):
    rows = []
    for t in (a, b):
        s = jnp.broadcast_to(jnp.sum(t, axis=1, keepdims=True), (NP, 128))
        rows.append(jnp.transpose(s)[0:1, :])
    return jnp.concatenate(rows, axis=1)


def keep_kernel(src, dst, sem):
    copy = pltpu.make_async_copy(src, dst, sem)
    copy.start()
    copy.wait()


def keep(a):
    return pl.pallas_call(
        keep_kernel,
        out_shape=pltpu.VMEM(a.shape, a.dtype),
        in_specs=[pl.BlockSpec(memory_space=pltpu.HBM)],
        out_specs=pl.BlockSpec(memory_space=pltpu.VMEM),
        scratch_shapes=[pltpu.SemaphoreType.DMA],
        compiler_params=params(12),
        cost_estimate=pl.CostEstimate(flops=0, bytes_accessed=2 * a.size * 2, transcendentals=0),
        name="keep",
    )(a)


def nt_kernel(steps, other, kept, with_sums, first_add, stacked, info, lhs_ref, rhs_ref, *refs):
    refs = list(refs)
    s_ref = refs.pop(0) if with_sums else None
    add_ref = refs.pop(0) if first_add is not None else None
    core = 1 - info[3] if other else info[3]
    n = len(steps)
    rows = [pl.ds(pl.multiple_of((2 * ((info[2] + k) % NX) + core) * W, W), W) for k in steps]
    if not kept:
        buf, sem = refs[-2:]
        copies = [pltpu.make_async_copy(rhs_ref.at[rows[i], :], buf.at[i], sem.at[i]) for i in range(n)]
        for cp in copies:
            cp.start()
    for i in range(n):
        if not kept:
            copies[i].wait()
        out = refs[0].at[i] if stacked else refs[i]
        acc = dot(lhs_ref[...], rhs_ref[rows[i], :] if kept else buf[i], NT)
        if first_add is not None:
            acc = acc + add_ref[first_add + i, :NP, :].astype(F32)
        out[:NP, :] = acc.astype(BF)
        if with_sums:
            if first_add is not None:
                out[NP:, :] = ride(unride(s_ref[...]) + unride(add_ref[first_add + i, NP:, :]))
            else:
                out[NP:, :] = s_ref[...]


def nt_call(steps, other, kept, info, lhs, rhs, sums=None, add=None, first_add=None, stacked=False, name=None):
    n = len(steps)
    rows = EXT if sums is not None else NP
    args = [info, lhs, rhs if kept else hbm(rhs)]
    in_specs = [SM, VM, VM if kept else pl.BlockSpec(memory_space=pltpu.HBM)]
    for extra in (sums, add):
        if extra is not None:
            args.append(extra)
            in_specs.append(VM)
    return pl.pallas_call(
        functools.partial(nt_kernel, steps, other, kept, sums is not None, first_add, stacked),
        in_specs=in_specs,
        out_specs=VM if stacked else tuple([VM] * n),
        out_shape=sds((n, rows, W), BF) if stacked else tuple([sds((rows, W), BF)] * n),
        scratch_shapes=[] if kept else [pltpu.VMEM((n, W, HID), BF), pltpu.SemaphoreType.DMA((n,))],
        compiler_params=params(BIG),
        cost_estimate=pl.CostEstimate(flops=2 * NP * HID * W * n, bytes_accessed=n << 20, transcendentals=0),
        name=name,
    )(*args)


def half_kernel(a_ref, b_ref, out_ref):
    out_ref[:NP, :] = a_ref[:NP, :].astype(F32) + b_ref[:NP, :].astype(F32)
    if a_ref.shape[0] > NP:
        at = lax.broadcasted_iota(jnp.int32, (16, W), 0)
        out_ref[NP:, :] = jnp.where(at == 0, unride(a_ref[NP:, :]) + unride(b_ref[NP:, :]), 0.0)


def tensor_scatter(info, lhs, rhs, sums, name, kept):
    o = send(nt_call((2, 1, 3, 0), True, kept, info, lhs, rhs, sums, stacked=True, name=name + "_o"), "c", 1)
    far, = nt_call((2,), False, kept, info, lhs, rhs, sums, o, 0, name=name + "_f")
    lhs, far = lax.optimization_barrier((lhs, far))
    far = send(far, "x", 2)
    ahead, behind, own = nt_call((1, 3, 0), False, kept, info, lhs, rhs, sums, o, 1, name=name + "_n")
    return call(half_kernel, sds(own.shape, F32), 0, 2, mib=BIG, nbytes=1 << 20, name=name + "_p")(own, far), send(
        ahead, "x", 1), send(behind, "x", -1)


def rows_kernel(x_ref, out_ref):
    row = lax.broadcasted_iota(jnp.int32, (256, 128), 0)
    col = lax.broadcasted_iota(jnp.int32, (256, 128), 1)
    pixel = 16 * (row // 32) + 2 * (row % 32 // 4) + row % 4
    chosen = jnp.where((col == pixel) & (row % 4 < 2), 1.0, 0.0).astype(BF)
    got = dot(chosen, x_ref[...], NT)
    at = lax.broadcasted_iota(jnp.int32, (256, NP), 0)
    out_ref[...] = jnp.where(at % 4 < 2, got, 1.0).astype(BF)


def bwd_kernel(own_ref, p1_ref, p2_ref, agg_ref, st_ref, gain_ref, g_ref, emb_ref, attn_ref, x_ref, q_ref,
               *rest):
    out_ref, acc, gq = rest
    parts = (own_ref, p1_ref, p2_ref)
    expand = head_mask(BF)
    scale = HEAD ** -0.5
    qrow = q_ref[...].astype(F32) * scale
    gain = gain_ref[...].astype(F32)
    sums = sum(unride(p[NP:, :]) for p in parts)
    cols = []
    for k in range(2):
        row = sums[:, k * NP:(k + 1) * NP] * (1.0 / D)
        cols.append(jnp.transpose(jnp.broadcast_to(row, (128, NP))))
    expand2 = jnp.concatenate([expand, expand], axis=0)
    rows = NP
    group = lane_group((rows, 128))
    group2 = lax.broadcasted_iota(jnp.int32, (rows, 256), 1) % 128 // 16
    for r in range(NP // rows):
        at = slice(r * rows, (r + 1) * rows)
        mean, inv = st_ref[0, at, 0:1], st_ref[1, at, 0:1]
        xh = (agg_ref[at, :].astype(F32) - mean) * inv
        gs = sum(p[at, :].astype(F32) for p in parts) * gain
        ga = g_ref[at, :].astype(F32) + inv * (gs - cols[0][at, 0:1] - xh * cols[1][at, 0:1])
        gab = ga.astype(BF).astype(F32)
        gattn = jnp.zeros((rows, 128), F32)
        for j in range(VMAX):
            prod = gab * emb_ref[j, at, :].astype(F32)
            hi = prod.astype(BF)
            low = (prod - hi.astype(F32)).astype(BF)
            both = dot(jnp.concatenate([hi, low], axis=0), expand, NT)
            both = both[:rows] + both[rows:]
            gattn = jnp.where(group == j, both, gattn)
        attn = attn_ref[at, :]
        gscore = attn * (gattn - over_slots(jnp.add, attn * gattn))
        ahi = attn.astype(BF)
        alow = (attn - ahi.astype(F32)).astype(BF)
        shi = gscore.astype(BF)
        slow = (gscore - shi.astype(F32)).astype(BF)
        a2 = jnp.concatenate([ahi, alow], axis=1)
        s2 = jnp.concatenate([shi, slow], axis=1)
        zero = jnp.zeros_like(a2)
        gst = jnp.transpose(shi.astype(F32)).astype(BF)
        for j in range(VMAX):
            pick = group2 == j
            wide = dot(jnp.concatenate([jnp.where(pick, a2, zero), jnp.where(pick, s2, zero)], axis=0), expand2)
            a_w, s_w = wide[:rows], wide[rows:]
            ge = (a_w * ga + s_w * qrow).astype(BF)
            mine = slice(16 * j, 16 * j + 16)
            part_q = dot(gst[mine, :], emb_ref[j, at, :])
            gq[mine, :] = part_q if r == 0 else gq[mine, :] + part_q
            got = dot(x_ref[32 * j:32 * j + 32, at], ge)
            for z in range(NZ):
                to = slice(32 * z + 4 * j, 32 * z + 4 * j + 4)
                if r == 0:
                    acc[to, :] = got[4 * z:4 * z + 4]
                else:
                    acc[to, :] += got[4 * z:4 * z + 4]
    total_q = jnp.sum(gq[...] * expand.astype(F32), axis=0, keepdims=True) * scale
    for z in range(NZ):
        acc[32 * z + 3:32 * z + 4, :] = total_q
        for y in range(NY):
            out_ref[NZ * y + z] = acc[32 * z:32 * z + 32, 128 * y:128 * y + 128].astype(BF)


def attention_backward(gn, agg, st, gain, g, emb, attn, x, q):
    return call(
        bwd_kernel, sds((NY * NZ, 32, 128), BF), 0, 11, [pltpu.VMEM((256, W), F32), pltpu.VMEM((128, W), F32)], mib=BIG,
        flops=2 * 6 * 8 * 256 * 128 * 512, nbytes=5 << 20, name="attn_bwd",
    )(gn[0], *map(hbm, gn[1:]), agg, st, gain, hbm(g), emb, attn, x, q)


def sum_kernel(destination, counts, ids, got_ref, main_ref, rest_ref, acc, bias, pair, query, inverse):
    acc[...] = jnp.zeros_like(acc)
    for i in range(NY * NZ):
        inverse[destination[i]] = i
    total = jnp.zeros((8, 128), F32)
    for rank in range(NY * NZ):
        sample = inverse[rank]
        live = counts[sample]
        data = got_ref[rank].astype(F32)
        total = total + data[0:8]
        for j in range(VMAX):
            v = jnp.where(j < live, ids[sample * VMAX + j], NVAR)
            acc[v, 0:4, :] += data[4 * j:4 * j + 4]
    query[...] = total
    for v in range(NVAR):
        pair[2 * v:2 * v + 2, :] = acc[v, 0:2, :]
        bias[v:v + 1, :] = acc[v, 2:3, :]
    for z in range(NZ):
        main_ref[z] = pair[...].astype(BF)
    rest_ref[0:48, :] = bias[...].astype(BF)
    rest_ref[48:64, :] = jnp.broadcast_to(query[3:4, :], (16, 128)).astype(BF)


def spread_kernel(info, *refs):
    pieces = refs[0:4]
    ge_ref, gv_ref, gq_ref, pair = refs[4:]
    for k, piece in enumerate(pieces):
        col = pl.ds(pl.multiple_of((info[0] + (0, 3, 1, 2)[k]) % NY * 128, 128), 128)
        for z in range(NZ):
            pair[...] = piece[96 * z:96 * z + 96, :].astype(F32)
            for v in range(NVAR):
                ge_ref[v, 2 * z:2 * z + 2, col] = pair[2 * v:2 * v + 2, :]
        gv_ref[:, col] = piece[768:816, :].astype(F32)
        gq_ref[:, col] = piece[816:832, :].astype(F32)[0:1]


def gradient_exchange(info, routing, outs):
    got = lax.all_to_all(outs, ("y", "z"), 0, 0, tiled=True)
    main, rest = call(
        sum_kernel, (sds((NZ, 96, 128), BF), sds((64, 128), BF)), 3, 1,
        [pltpu.VMEM((NVAR + 1, 8, 128), F32), pltpu.VMEM((NVAR, 128), F32), pltpu.VMEM((96, 128), F32),
         pltpu.VMEM((8, 128), F32), pltpu.SMEM((NY * NZ,), jnp.int32)],
        mib=BIG, flops=1 << 20, nbytes=2 << 20, name="slot_sum",
    )(*routing, got)
    main = lax.all_to_all(main, "z", 0, 0, tiled=True)
    both = jnp.concatenate([main.reshape(NZ * 96, 128), rest], axis=0)
    pieces = [both, send(both, "y", 1), send(both, "y", -1), send(both, "y", 2)]
    return call(
        spread_kernel, (sds((NVAR, PP, W), F32), sds((NVAR, W), F32), sds((1, W), F32)), 1, 4,
        [pltpu.VMEM((96, 128), F32)], mib=BIG, flops=1 << 20, nbytes=3 << 20, name="spread",
    )(info, both, *map(hbm, pieces[1:]))


def mix_kernel(agg_ref, own, p1, p2, out_ref):
    total = agg_ref[:NP, :].astype(F32)
    for p in (own, p1, p2):
        total = total + p[...].astype(F32)
    out_ref[0] = total.astype(BF)


def pixel_gather(own):
    mine = jnp.stack([own, send(own, "x", 1), send(own, "x", -1), send(own, "x", 2)])
    return mine, send(mine, "c", 1)


def local(pixels, counts, var_ids, destination, embed_weight, var_embed, agg_query, ln_gain, fc_up, fc_down, cotangent):
    y, z, x, c = (lax.axis_index(a) for a in ("y", "z", "x", "c"))
    info = jnp.stack([y, z, x, c]).astype(jnp.int32)
    routing = destination, counts, var_ids.reshape(-1)
    g_own = cotangent[0]
    down = lax.all_gather(fc_down, ("y", "z"), axis=0, tiled=True)

    to_rank = destination[None, :] == jnp.arange(NY * NZ)[:, None]
    ordered = dot(to_rank.astype(BF), pixels[:, 0, :]).astype(BF)
    mine = lax.all_to_all(ordered, ("y", "z"), 0, 0, tiled=True)
    q, info, mine = lax.optimization_barrier((agg_query.reshape(1, W), info, mine))
    mine, swapped = pixel_gather(mine)

    agg, emb, attn, patches = attention_forward(info, routing, (mine, swapped), embed_weight, var_embed, q, ln_gain)
    pieces = tensor_gather(agg)
    pre, dg, hid, u, st = up_call(info, pieces, fc_up)
    g_late, _ = lax.optimization_barrier((g_own, u))
    g_pieces = tensor_gather(g_late)
    up_src, _ = lax.optimization_barrier((fc_up, g_pieces[4]))
    up_kept = keep(up_src)
    rows = call(rows_kernel, sds((256, NP), BF), 0, 1, mib=BIG, nbytes=1 << 20, name="rows")(patches)
    down, up_kept, g_whole, rows = lax.optimization_barrier((down, up_kept, join(info, g_pieces), rows))
    gp, sums = grad_pre(g_whole, down, pre, dg, u)
    gn = tensor_scatter(info, gp, up_kept, sums, "gn", True)
    mark, _ = lax.optimization_barrier((sums, gn[0]))
    hid, _ = lax.optimization_barrier((hid, send(mark, "c", 1)))
    br = tensor_scatter(info, hid, down, None, "br", False)
    outs = attention_backward(gn, agg, st, ln_gain, g_own, emb, attn, rows, q)
    mixed = call(mix_kernel, sds((1, NP, W), BF), 0, 4, mib=BIG, nbytes=1 << 20, name="mix")(
        agg, br[0], *map(hbm, br[1:]))
    ge, gv, gq = gradient_exchange(info, routing, outs)
    return mixed, ge, gv, gq.reshape(W)


def solution(mesh):
    fine = Mesh(mesh.devices.reshape(NY, NZ, NX, NC), ("y", "z", "x", "c"))
    dp, tensor = ("y", "z"), ("x", "c")
    in_specs = (
        P(None, dp + tensor, None), P(), P(), P(), P(None, None, tensor), P(None, tensor), P(tensor),
        P(None, tensor), P(None, tensor), P(dp, tensor), P(dp, None, tensor),
    )
    out_specs = (P(dp, None, tensor), P(None, None, tensor), P(None, tensor), P(tensor))
    return jax.shard_map(local, mesh=fine, in_specs=in_specs, out_specs=out_specs, check_vma=False)
```
